32 devices in a mesh: dp: 4 (over y, x), shard: 8 (over z, core).
Axes of the slice: x: 2, y: 2, z: 4, core: 2. Of those that a mesh axis runs over, the one named last changes fastest.
Arguments:
- activations: bfloat16 [32, 256, 1024], P(('dp', 'shard')), may hold values from -120 to 120
- out_grad: bfloat16 [32, 256, 1024], P(('dp', 'shard')), may hold values from -6 to 6
- weights: bfloat16 [256, 27, 256], P('shard'), may hold values from -0.078125 to 0.078125
Outputs:
- activated: bfloat16 [32, 256, 1024], P(('dp', 'shard'))
- update: float32 [256, 27, 256], P('shard')
The draws below stay inside these ranges and needn't reach their ends.
All inputs are finite; a program needn't handle non-finite values.
Results may differ from the reference program's by a relative error of at most 0.0026.
Values may be sent and summed in bfloat16 or wider, within the bound.
No kernel may reach another device: no remote copies, remote signals or barrier semaphores. Data moves between devices by JAX's collectives and lax.ppermute only.
A program may use at most 128 MiB of HBM per device.

```python
import math
import jax
import jax.numpy as jnp
from jax import lax

C = 256
TAPS = 27
SX = 4
SY = 16
SZ = 16
NS_ITERS = 8
CELLS = 1024
SAMPLES = 32


def draw_activations(key, part):
    key_chan, key_base = jax.random.split(key)
    channel_scale = jnp.exp(jax.random.uniform(key_chan, (1, C, 1), jnp.float32, 0.0, math.log(10.0)))
    ramp = jnp.arange(SAMPLES, dtype=jnp.float32) / max(SAMPLES - 1, 1)
    sample_scale = jnp.exp(math.log(3.0) * ramp).reshape(SAMPLES, 1, 1)
    base = jnp.clip(jax.random.normal(key_base, (SAMPLES, C, CELLS), jnp.float32), -4.0, 4.0)
    return (base * channel_scale * sample_scale).astype(jnp.bfloat16)


def steps_of(key, extent, pieces, smallest, high):
    loudness = 1.0
    for dim, shards_of in pieces:
        heights = jax.random.uniform(jax.random.fold_in(jax.random.fold_in(key, 6), dim), (shards_of,), jnp.float32, smallest / len(pieces), high / len(pieces))
        loudness = loudness * jnp.repeat(jnp.exp(heights), extent[dim] // shards_of).reshape((-1,) + (1,) * (len(extent) - 1 - dim))
    return loudness


def bell_draw(rng, shape, width, reach, pieces=(), kind=jnp.bfloat16):
    values = jax.random.normal(rng, shape, jnp.float32) * width
    if len(pieces) > 0:
        values = steps_of(rng, shape, pieces, -0.22, 0.18) * values
    return jnp.clip(values, min=-reach, max=reach).astype(kind)


def setup_inputs(seed: int = 0) -> dict:
    key_of = jax.random.split(jax.random.key(seed), 4)
    return {
        "activations": draw_activations(jax.random.fold_in(key_of[3], 71), 0),
        "out_grad": bell_draw(key_of[1], (SAMPLES, C, CELLS), 1.0, 6.0, ((0, 32),)),
        "weights": bell_draw(key_of[2], (C, TAPS, C), (TAPS * C) ** -0.5, 0.078125, ((0, 8),)),
    }


DAMPING = 0.001

def shift_cells(values, offset):
    height = values.shape[0]
    cube = values.reshape(height, SX, SY, SZ)
    padded = jnp.pad(cube, ((0, 0), (1, 1), (1, 1), (1, 1)))
    along_x = offset // 9
    along_y = offset // 3 % 3
    along_z = offset % 3
    window = padded[:, along_x:along_x + SX, along_y:along_y + SY, along_z:along_z + SZ]
    return window.reshape(height, SX * SY * SZ)

def newton_inverse(matrix):
    identity = jnp.eye(matrix.shape[0], dtype=jnp.float32)
    approx = identity / jnp.trace(matrix)
    for sweep in range(NS_ITERS):
        inner = jnp.dot(matrix, approx, precision=lax.Precision.HIGHEST)
        approx = jnp.dot(approx, 2.0 * identity - inner, precision=lax.Precision.HIGHEST)
    return approx

def reference(activations, out_grad, weights):

    def one_sample(carry, sample):
        a_sum, g_sum, grad_sum = carry
        inputs, cotangent = sample
        shifted = [shift_cells(inputs, offset) for offset in range(TAPS)]
        outputs = jnp.zeros((C, CELLS), jnp.float32)
        for offset in range(TAPS):
            outputs = outputs + jnp.dot(weights[:, offset, :].T, shifted[offset], preferred_element_type=jnp.float32)
        sigma = jax.nn.sigmoid(outputs)
        result = (outputs * sigma).astype(jnp.bfloat16)
        slope = (cotangent.astype(jnp.float32) * sigma * (1.0 + outputs * (1.0 - sigma))).astype(jnp.bfloat16)
        a_sum = a_sum + jnp.dot(inputs, inputs.T, preferred_element_type=jnp.float32)
        g_sum = g_sum + jnp.dot(slope, slope.T, preferred_element_type=jnp.float32)
        term = jnp.stack([jnp.dot(shifted[offset], slope.T, preferred_element_type=jnp.float32) for offset in range(TAPS)], axis=1)
        return ((a_sum, g_sum, grad_sum + term), result)
    start = (jnp.zeros((C, C), jnp.float32), jnp.zeros((C, C), jnp.float32), jnp.zeros((C, TAPS, C), jnp.float32))
    (a_sum, g_sum, grad_sum), activated = lax.scan(one_sample, start, (activations, out_grad))
    total = SAMPLES * CELLS
    identity = jnp.eye(C, dtype=jnp.float32)
    inv_a = newton_inverse(a_sum / total + DAMPING * identity)
    inv_g = newton_inverse(g_sum / total + DAMPING * identity)
    scale = 1.0 / math.sqrt(total)
    product = jnp.dot(inv_a, grad_sum.reshape(C, TAPS * C), precision=lax.Precision.HIGHEST)
    update = jnp.dot(product.reshape(C * TAPS, C), inv_g, precision=lax.Precision.HIGHEST) * scale
    return (activated, update.reshape(C, TAPS, C))
```

```python
import functools
import math

import jax
import jax.numpy as jnp
from jax import lax
from jax.experimental import pallas as pl
from jax.experimental.pallas import tpu as pltpu
from jax.sharding import PartitionSpec as P

SX = 4
SY = 16
SZ = 16
NS_ITERS = 8
DAMPING = 0.001
AXES = ("dp", "shard")
NT = (((1,), (1,)), ((), ()))


def exchange(x, planes, pairs, dp=0, z=0, core=0):
    perm = []
    for a in range(planes):
        for b in range(pairs):
            for c in range(2):
                here = (a * pairs + b) * 2 + c
                there = ((a ^ dp) * pairs + (b ^ z)) * 2 + (c ^ core)
                perm.append((here, there))
    return lax.ppermute(x, AXES, perm)


def rows_of(x, index, height):
    return lax.dynamic_slice_in_dim(x, index * height, height, 0)


def place(buffer, block, index):
    return lax.dynamic_update_slice_in_dim(buffer, block, index * block.shape[0], 0)


def by_core(core, mine, other):
    return jnp.where(
        core == 0, jnp.concatenate([mine, other]), jnp.concatenate([other, mine])
    )


def newton_inverse(matrix):
    identity = jnp.eye(matrix.shape[0], dtype=jnp.float32)
    approx = identity / jnp.trace(matrix)
    for sweep in range(NS_ITERS):
        inner = jnp.dot(matrix, approx, precision=lax.Precision.HIGHEST)
        approx = jnp.dot(approx, 2.0 * identity - inner, precision=lax.Precision.HIGHEST)
    return approx


def stage_kernel(first, taps, out, *refs):
    kernel, act0, act1, cot0, cot1 = refs[:5]
    refs = refs[5:]
    total_in = None
    if not first:
        total_in, refs = refs[0], refs[1:]
    total, act_out0, act_out1, slope0, slope1, wide, moved = refs
    cells = act0.shape[1]
    lane = lax.broadcasted_iota(jnp.int32, (out, cells), 1)
    spots = (lane // (SY * SZ), lane // SZ % SY, lane % SZ)
    strides = (SY * SZ, SZ, 1)
    sizes = (SX, SY, SZ)

    def shifted(value, dim, step):
        if step == 0:
            return value
        moved_by = pltpu.roll(value, (-step * strides[dim]) % cells, 1)
        inside = spots[dim] < sizes[dim] - 1 if step > 0 else spots[dim] > 0
        return jnp.where(inside, moved_by, 0.0)

    for window, (act, cot, act_out, slope_out) in enumerate(
        ((act0, cot0, act_out0, slope0), (act1, cot1, act_out1, slope1))
    ):
        inputs = act[...]
        wide[...] = jnp.dot(kernel[...], inputs, preferred_element_type=jnp.float32)
        outputs = None
        for a in range(3):
            over_b = None
            for b in range(3):
                over_c = None
                for c in range(3):
                    tap = 9 * a + 3 * b + c
                    part = shifted(wide[tap * out : (tap + 1) * out, :], 2, c - 1)
                    over_c = part if over_c is None else over_c + part
                part = shifted(over_c, 1, b - 1)
                over_b = part if over_b is None else over_b + part
            part = shifted(over_b, 0, a - 1)
            outputs = part if outputs is None else outputs + part
        sigma = jax.nn.sigmoid(outputs)
        act_out[...] = (outputs * sigma).astype(jnp.bfloat16)
        slope = (
            cot[...].astype(jnp.float32) * sigma * (1.0 + outputs * (1.0 - sigma))
        ).astype(jnp.bfloat16)
        slope_out[...] = slope
        slope = slope.astype(jnp.float32)
        for a in range(3):
            at_a = shifted(slope, 0, 1 - a)
            for b in range(3):
                at_b = shifted(at_a, 1, 1 - b)
                for c in range(3):
                    tap = 9 * a + 3 * b + c
                    moved[tap * out : (tap + 1) * out, :] = shifted(at_b, 2, 1 - c).astype(
                        jnp.bfloat16
                    )
        moved[taps * out :, :] = inputs
        sums = lax.dot_general(moved[...], inputs, NT, preferred_element_type=jnp.float32)
        if window == 0:
            total[...] = sums if first else total_in[...] + sums
        else:
            total[...] += sums


def run_stage(kernel, acts, cots, total, taps, out):
    channels, cells = acts[0].shape
    rows = taps * out + channels
    first = total is None
    args = [kernel, *acts, *cots] + ([] if first else [total])
    small = jax.ShapeDtypeStruct((out, cells), jnp.bfloat16)
    flops = 2 * 2 * cells * channels * (taps * out + rows)
    return pl.pallas_call(
        functools.partial(stage_kernel, first, taps, out),
        out_shape=[jax.ShapeDtypeStruct((rows, channels), jnp.float32)] + [small] * 4,
        in_specs=[pl.BlockSpec(memory_space=pltpu.VMEM)] * len(args),
        out_specs=[pl.BlockSpec(memory_space=pltpu.VMEM)] * 5,
        scratch_shapes=[
            pltpu.VMEM((taps * out, cells), jnp.float32),
            pltpu.VMEM((rows, cells), jnp.bfloat16),
        ],
        input_output_aliases={} if first else {5: 0},
        compiler_params=pltpu.CompilerParams(vmem_limit_bytes=32 * 1024 * 1024),
        cost_estimate=pl.CostEstimate(
            flops=flops, bytes_accessed=4 * 1024 * 1024, transcendentals=4 * out * cells
        ),
    )(*args)


def shards(planes, pairs, activations, out_grad, weights):
    inputs = activations[0]
    cotangent = out_grad[0]
    channels, cells = inputs.shape
    own_rows, taps, _ = weights.shape
    out = channels // (2 * planes)
    my_plane = lax.axis_index("dp")
    my_index = lax.axis_index("shard")
    my_pair = my_index // 2
    my_core = my_index % 2
    swap = functools.partial(exchange, planes=planes, pairs=pairs)

    columns = lax.dynamic_slice_in_dim(weights, my_plane * 2 * out, 2 * out, 2)
    mine = lax.dynamic_slice_in_dim(columns, my_core * out, out, 2)
    other = lax.dynamic_slice_in_dim(columns, (1 - my_core) * out, out, 2)
    mine = mine.reshape(own_rows, taps * out)
    other = swap(other.reshape(own_rows, taps * out), core=1)
    block = by_core(my_core, mine, other)
    kernel = jnp.zeros((channels, taps * out), jnp.bfloat16)
    for step in range(pairs):
        part = block if step == 0 else swap(block, z=step)
        kernel = place(kernel, part, my_pair ^ step)
    kernel = kernel.T

    total = None
    activated = jnp.zeros((channels, cells), jnp.bfloat16)
    slopes = jnp.zeros((channels, cells), jnp.bfloat16)
    for step in range(planes):
        act = inputs if step == 0 else swap(inputs, dp=step)
        cot = rows_of(cotangent, my_plane ^ step, 2 * out)
        cot = cot if step == 0 else swap(cot, dp=step)
        act_pair = (act, swap(act, core=1))
        cot_pair = (rows_of(cot, my_core, out), swap(rows_of(cot, 1 - my_core, out), core=1))
        total, act0, act1, slope0, slope1 = run_stage(
            kernel, act_pair, cot_pair, total, taps, out
        )
        back = by_core(my_core, slope0, swap(slope1, core=1))
        back = back if step == 0 else swap(back, dp=step)
        slopes = place(slopes, back, my_plane ^ step)
        back = by_core(my_core, act0, swap(act1, core=1))
        back = back if step == 0 else swap(back, dp=step)
        activated = place(activated, back, my_plane ^ step)

    samples = planes * pairs * 2
    count = samples * cells
    identity = jnp.eye(channels, dtype=jnp.float32)
    half = channels // 2

    gram = total[taps * out :]
    part = rows_of(gram, my_core, half)
    a_half = part
    for step in range(1, pairs):
        a_half = a_half + swap(part, z=step)
    a_sum = by_core(my_core, a_half, swap(a_half, core=1))
    inv_a = newton_inverse(a_sum / count + DAMPING * identity)

    gram = jnp.dot(slopes, slopes.T, preferred_element_type=jnp.float32)
    g_half = rows_of(gram, my_core, half) + swap(rows_of(gram, 1 - my_core, half), core=1)
    piece = half // planes
    part = rows_of(g_half, my_plane, piece)
    for step in range(1, planes):
        part = part + swap(rows_of(g_half, my_plane ^ step, piece), dp=step)
    over_z = part
    for step in range(1, pairs):
        over_z = over_z + swap(part, z=step)
    g_half = jnp.zeros((half, channels), jnp.float32)
    for step in range(planes):
        part = over_z if step == 0 else swap(over_z, dp=step)
        g_half = place(g_half, part, my_plane ^ step)
    g_sum = by_core(my_core, g_half, swap(g_half, core=1))
    inv_g = newton_inverse(g_sum / count + DAMPING * identity)

    product = lax.dot_general(inv_a, total[: taps * out], NT, precision=lax.Precision.HIGHEST)
    narrow = product.astype(jnp.bfloat16)
    rows = rows_of(product, my_pair, 2 * own_rows)
    for step in range(1, pairs):
        part = swap(rows_of(narrow, my_pair ^ step, 2 * own_rows), z=step)
        rows = rows + part.astype(jnp.float32)
    mine = rows_of(rows, my_core, own_rows)
    other = swap(rows_of(rows, 1 - my_core, own_rows), core=1)
    block = by_core(my_core, mine, other)
    full = jnp.zeros((channels // out * own_rows, taps * out), jnp.float32)
    for step in range(planes):
        part = block if step == 0 else swap(block, dp=step)
        full = place(full, part, my_plane ^ step)
    full = full.reshape(channels // out, own_rows, taps, out).transpose(2, 1, 0, 3)
    scale = 1.0 / math.sqrt(count)
    update = (
        jnp.dot(full.reshape(taps * own_rows, channels), inv_g, precision=lax.Precision.HIGHEST)
        * scale
    )
    update = update.reshape(taps, own_rows, channels).transpose(1, 0, 2)
    return activated[None], update


def solution(mesh):
    planes = mesh.shape["dp"]
    pairs = mesh.shape["shard"] // 2
    return jax.shard_map(
        functools.partial(shards, planes, pairs),
        mesh=mesh,
        in_specs=(
            P(("dp", "shard"), None, None),
            P(("dp", "shard"), None, None),
            P("shard", None, None),
        ),
        out_specs=(P(("dp", "shard"), None, None), P("shard", None, None)),
        check_vma=False,
    )
```

```python
import functools
import math

import jax
import jax.numpy as jnp
from jax import lax
from jax.experimental import pallas as pl
from jax.experimental.pallas import tpu as pltpu
from jax.sharding import PartitionSpec as P

SX = 4
SY = 16
SZ = 16
NS_ITERS = 8
DAMPING = 0.001
AXES = ("dp", "shard")
NT = (((1,), (1,)), ((), ()))
VMEM = pl.BlockSpec(memory_space=pltpu.VMEM)
SMEM = pl.BlockSpec(memory_space=pltpu.SMEM)
PARAMS = pltpu.CompilerParams(vmem_limit_bytes=32 * 1024 * 1024)


def exchange(x, planes, pairs, dp=0, z=0, core=0):
    perm = []
    for a in range(planes):
        for b in range(pairs):
            for c in range(2):
                here = (a * pairs + b) * 2 + c
                there = ((a ^ dp) * pairs + (b ^ z)) * 2 + (c ^ core)
                perm.append((here, there))
    return lax.ppermute(x, AXES, perm)


def after(x, *others):
    return lax.optimization_barrier((x, *others))[0]


def rows_of(x, index, height):
    return lax.dynamic_slice_in_dim(x, index * height, height, 0)


def place(buffer, block, index):
    return lax.dynamic_update_slice_in_dim(buffer, block, index * block.shape[0], 0)


def by_core(core, mine, other):
    return jnp.where(
        core == 0, jnp.concatenate([mine, other]), jnp.concatenate([other, mine])
    )


def dot3(left, right):
    left_high = left.astype(jnp.bfloat16)
    left_low = (left - left_high.astype(jnp.float32)).astype(jnp.bfloat16)
    right_high = right.astype(jnp.bfloat16)
    right_low = (right - right_high.astype(jnp.float32)).astype(jnp.bfloat16)

    def dot(a, b):
        return jnp.dot(a, b, preferred_element_type=jnp.float32)

    return dot(left_high, right_high) + (dot(left_high, right_low) + dot(left_low, right_high))


def shifter(shape):
    cells = shape[1]
    lane = lax.broadcasted_iota(jnp.int32, shape, 1)
    spots = (lane // (SY * SZ), lane // SZ % SY, lane % SZ)
    strides = (SY * SZ, SZ, 1)
    sizes = (SX, SY, SZ)

    def shifted(value, dim, step):
        if step == 0:
            return value
        rolled = pltpu.roll(value, (-step * strides[dim]) % cells, 1)
        inside = spots[dim] < sizes[dim] - 1 if step > 0 else spots[dim] > 0
        return jnp.where(inside, rolled, 0.0)

    return shifted


def columns_kernel(pairs, at, *refs):
    blocks, (result, rows) = refs[:pairs], refs[pairs:]
    height = blocks[0].shape[0]
    for step in range(pairs):
        start = pl.multiple_of((at[0] ^ step) * height, height)
        rows[pl.ds(start, height), :] = blocks[step][...].astype(jnp.float32)
    result[...] = rows[...].T.astype(jnp.bfloat16)


def forward_kernel(taps, out, parts, core, kernel, *refs):
    windows = (refs[:parts], refs[parts : 2 * parts])
    results, (inputs, wide) = refs[2 * parts : -2], refs[-2:]
    slope_out = results[0]
    act_out = results[0].at[2 * out :] if len(results) == 1 else results[1]
    channels, cells = inputs.shape[1:]
    shifted = shifter((out, cells))
    for window, pieces in enumerate(windows):
        cot = gather_window(channels, out, core, pieces, inputs.at[window])
        wide[...] = jnp.dot(kernel[...], inputs[window], preferred_element_type=jnp.float32)
        outputs = None
        for a in range(3):
            over_b = None
            for b in range(3):
                over_c = None
                for c in range(3):
                    tap = 9 * a + 3 * b + c
                    part = shifted(wide[tap * out : (tap + 1) * out, :], 2, c - 1)
                    over_c = part if over_c is None else over_c + part
                part = shifted(over_c, 1, b - 1)
                over_b = part if over_b is None else over_b + part
            part = shifted(over_b, 0, a - 1)
            outputs = part if outputs is None else outputs + part
        sigma = jax.nn.sigmoid(outputs)
        cot = cot.astype(jnp.float32)
        act_out[window * out : (window + 1) * out, :] = (outputs * sigma).astype(jnp.bfloat16)
        slope_out[window * out : (window + 1) * out, :] = (
            cot * sigma * (1.0 + outputs * (1.0 - sigma))
        ).astype(jnp.bfloat16)


def gather_window(channels, out, core, pieces, inputs):
    start = 0
    for piece in pieces:
        height = min(piece.shape[0], channels - start)
        if height > 0:
            inputs[start : start + height, :] = piece[:height, :]
            start += height
    last = pieces[-1]
    first = pl.multiple_of(last.shape[0] - 2 * out + core[0] * out, out)
    return last[pl.ds(first, out), :]


def gradient_kernel(first, taps, out, slopes, inputs, *refs):
    total_in = None if first else refs[0]
    total, moved = refs[-2:]
    channels, cells = inputs.shape[1:]
    shifted = shifter((out, cells))
    for window in range(2):
        slope = slopes[window * out : (window + 1) * out, :].astype(jnp.float32)
        for a in range(3):
            at_a = shifted(slope, 0, 1 - a)
            for b in range(3):
                at_b = shifted(at_a, 1, 1 - b)
                for c in range(3):
                    tap = 9 * a + 3 * b + c
                    moved[tap * out : (tap + 1) * out, :] = shifted(at_b, 2, 1 - c).astype(
                        jnp.bfloat16
                    )
        sums = lax.dot_general(
            moved[...], inputs[window], NT, preferred_element_type=jnp.float32
        )
        if window == 0:
            total[...] = sums if first else total_in[...] + sums
        else:
            total[...] += sums


def gram_kernel(planes, out, at, core, *refs):
    mine, theirs, (result, slopes) = refs[:planes], refs[planes : 2 * planes], refs[2 * planes :]
    half = result.shape[0]
    cells = mine[0].shape[1]
    own = pl.multiple_of(core[0] * half, half)
    other = pl.multiple_of((1 - core[0]) * half, half)
    for step in range(planes):
        plane = (at[0] ^ step) * out
        for window in range(2):
            columns = slice(window * cells, (window + 1) * cells)
            rows = slice(window * out, (window + 1) * out)
            slopes[pl.ds(pl.multiple_of(own + plane, out), out), columns] = mine[step][rows, :]
            rows = slice((1 - window) * out, (2 - window) * out)
            slopes[pl.ds(pl.multiple_of(other + plane, out), out), columns] = theirs[step][rows, :]
    result[...] = lax.dot_general(
        slopes[pl.ds(own, half), :], slopes[...], NT, preferred_element_type=jnp.float32
    )


def inputs_gram_kernel(core, mine, theirs, result):
    half, channels = result.shape
    own = pl.multiple_of(core[0] * half, half)
    result[...] = lax.dot_general(
        mine[pl.ds(own, half), :], mine[:channels, :], NT, preferred_element_type=jnp.float32
    ) + lax.dot_general(
        theirs[pl.ds(own, half), :], theirs[:channels, :], NT, preferred_element_type=jnp.float32
    )


def sort_kernel(planes, out, at, core, *refs):
    mine, theirs, result = refs[:planes], refs[planes:-1], refs[-1]
    half = result.shape[0] // 2
    for step in range(planes):
        plane = (at[0] ^ step) * out
        piece = mine[step]
        first = piece.shape[0] - 2 * out
        start = pl.multiple_of(core[0] * half + plane, out)
        result[pl.ds(start, out), :] = piece[first : first + out, :]
        start = pl.multiple_of((1 - core[0]) * half + plane, out)
        result[pl.ds(start, out), :] = theirs[step][first + out : first + 2 * out, :]


def newton_kernel(count, core, mine, theirs, result, matrix, both):
    half, size = mine.shape
    matrix[pl.ds(pl.multiple_of(core[0] * half, half), half), :] = mine[...]
    matrix[pl.ds(pl.multiple_of((1 - core[0]) * half, half), half), :] = theirs[...]
    row = lax.broadcasted_iota(jnp.int32, (size, size), 0)
    column = lax.broadcasted_iota(jnp.int32, (size, size), 1)
    identity = jnp.where(row == column, 1.0, 0.0)
    factor = matrix[...] / count + DAMPING * identity
    diagonal = jnp.sum(factor * identity, axis=1, keepdims=True)
    scale = 1.0 / jnp.sum(diagonal, axis=0, keepdims=True)
    error = identity - factor * scale
    both[:size, :] = (identity + error) * scale
    both[size:, :] = error
    for sweep in range(1, NS_ITERS):
        if sweep == 1:
            both[size:, :] = dot3(error, error)
        last = sweep == NS_ITERS - 1
        products = dot3(both[:size, :] if last else both[...], both[size:, :])
        both[:size, :] += products[:size]
        if not last:
            both[size:, :] = products[size:]
    result[...] = both[:size, :]


def update_kernel(planes, taps, out, scale, at, inverse, *refs):
    pieces, (result, rows, factor) = refs[:planes], refs[planes:]
    own_rows = pieces[0].shape[0] // 2
    half = inverse.shape[0] // 2
    for step in range(planes):
        for core in range(2):
            block = (step * 2 + core) * out
            start = pl.multiple_of(core * half + (at[0] ^ step) * out, out)
            factor[block : block + out, :] = inverse[pl.ds(start, out), :]
            for tap in range(taps):
                rows[tap * own_rows : (tap + 1) * own_rows, block : block + out] = pieces[step][
                    core * own_rows : (core + 1) * own_rows, tap * out : (tap + 1) * out
                ]
    result[...] = dot3(rows[...], factor[...]) * scale


def call(kernel, args, shapes, scratch, flops, scalars=0, aliases=None):
    moved = sum(a.size * a.dtype.itemsize for a in list(args) + list(shapes))
    return pl.pallas_call(
        kernel,
        out_shape=tuple(shapes),
        in_specs=[SMEM] * scalars + [VMEM] * (len(args) - scalars),
        out_specs=tuple([VMEM] * len(shapes)),
        scratch_shapes=scratch,
        input_output_aliases=aliases or {},
        compiler_params=PARAMS,
        cost_estimate=pl.CostEstimate(flops=flops, bytes_accessed=moved, transcendentals=0),
    )(*args)


def shards(planes, pairs, activations, out_grad, weights):
    f32, bf16 = jnp.float32, jnp.bfloat16
    shape = jax.ShapeDtypeStruct
    inputs = activations[0]
    cotangent = out_grad[0]
    channels, cells = inputs.shape
    own_rows, taps, _ = weights.shape
    out = channels // (2 * planes)
    half = channels // 2
    wide = taps * out
    my_plane = lax.axis_index("dp")
    my_index = lax.axis_index("shard")
    my_pair = my_index // 2
    my_core = my_index % 2
    at_plane = my_plane.reshape(1)
    at_pair = my_pair.reshape(1)
    at_core = my_core.reshape(1)
    swap = functools.partial(exchange, planes=planes, pairs=pairs)

    def kernel_columns(core):
        start = core * half + my_plane * out
        part = lax.dynamic_slice_in_dim(weights, start, out, 2)
        return part.reshape(own_rows, wide)

    def cotangent_rows(step):
        plane = my_plane ^ step
        first = rows_of(cotangent, plane, out)
        second = lax.dynamic_slice_in_dim(cotangent, half + plane * out, out, 0)
        return [first, second]

    block = by_core(my_core, kernel_columns(my_core), swap(kernel_columns(1 - my_core), core=1))
    blocks = [block] + [swap(block, z=step) for step in range(1, pairs)]
    (kernel,) = call(
        functools.partial(columns_kernel, pairs),
        (at_pair, *blocks),
        [shape((wide, channels), bf16)],
        [pltpu.VMEM((channels, wide), f32)],
        0,
        scalars=1,
    )

    own = jnp.concatenate([inputs, *cotangent_rows(0)])
    straight = [step for step in range(1, planes) if step & (step - 1) == 0]
    arrived = [
        swap(jnp.concatenate([inputs, *cotangent_rows(step)]), dp=step) for step in straight
    ]
    arrived = lax.optimization_barrier(tuple(arrived))
    windows = {0: [own], **{step: [part] for step, part in zip(straight, arrived)}}
    for step in range(1, planes):
        if step not in windows:
            low = step & -step
            high = (step ^ low) & -(step ^ low)
            by_high = windows[step ^ high]
            by_low = windows[step ^ low]
            first = by_high[0] if len(by_high) == 3 else by_high[0][:half]
            second = by_low[1] if len(by_low) == 3 else by_low[0][half:channels]
            cot = swap(jnp.concatenate(cotangent_rows(step)), dp=step)
            windows[step] = [swap(first, dp=high), swap(second, dp=low), cot]

    others = swap(own, core=1)
    (part,) = call(
        inputs_gram_kernel,
        (at_core, own, others),
        [shape((half, channels), f32)],
        [],
        2 * 2 * half * channels * cells,
        scalars=1,
    )
    part = after(part, *blocks)
    a_half = part
    for step in range(1, pairs):
        a_half = a_half + swap(part, z=step)

    total = None
    back = []
    theirs = []
    slope = None
    for step in range(planes):
        mine = windows[step]
        last = step == planes - 1
        if step > 0:
            tied = (slope, a_half) if last else (slope,)
            mine = [after(part, *tied) for part in mine]
            others = [swap(part, core=1) for part in mine]
        else:
            others = [others]
        heights = (2 * out, 2 * out) if last else (4 * out,)
        *results, pair = call(
            functools.partial(forward_kernel, taps, out, len(mine)),
            (at_core, kernel, *mine, *others),
            [shape((height, cells), bf16) for height in heights]
            + [shape((2, channels, cells), bf16)],
            [pltpu.VMEM((wide, cells), f32)],
            2 * 2 * wide * channels * cells,
            scalars=1,
        )
        slope = results[0]
        back.append(slope if step == 0 else swap(slope, dp=step))
        theirs.append(swap(back[-1], core=1))
        (total,) = call(
            functools.partial(gradient_kernel, step == 0, taps, out),
            (slope, pair) + (() if step == 0 else (total,)),
            [shape((wide, channels), f32)],
            [pltpu.VMEM((wide, cells), bf16)],
            2 * 2 * wide * channels * cells,
            aliases={} if step == 0 else {2: 0},
        )
    part = after(a_half, *windows[planes - 1])
    a_half = part
    for step in range(1, planes):
        a_half = a_half + swap(part, dp=step)

    count = planes * pairs * 2 * cells

    def inverse_of(mine):
        return call(
            functools.partial(newton_kernel, count),
            (at_core, mine, swap(mine, core=1)),
            [shape((channels, channels), f32)],
            [pltpu.VMEM((channels, channels), f32), pltpu.VMEM((2 * channels, channels), f32)],
            6 * NS_ITERS * 4 * channels**3,
            scalars=1,
        )[0]

    (g_half,) = call(
        functools.partial(gram_kernel, planes, out),
        (at_plane, at_core, *back, *theirs),
        [shape((half, channels), f32)],
        [pltpu.VMEM((channels, 2 * cells), bf16)],
        2 * 2 * half * channels * cells,
        scalars=2,
    )
    part = rows_of(g_half, my_plane, out)
    for step in range(1, planes):
        part = part + swap(rows_of(g_half, my_plane ^ step, out), dp=step)
    over_z = part
    for step in range(1, pairs):
        over_z = over_z + swap(part, z=step)
    g_half = jnp.zeros((half, channels), f32)
    for step in range(planes):
        part = over_z if step == 0 else swap(over_z, dp=step)
        g_half = place(g_half, part, my_plane ^ step)

    inv_a = inverse_of(a_half)
    inv_g = inverse_of(g_half)

    product = lax.dot_general(inv_a, total, NT, precision=lax.Precision.HIGHEST)
    narrow = product.astype(bf16)
    rows = rows_of(product, my_pair, 2 * own_rows)
    for step in range(1, pairs):
        part = swap(rows_of(narrow, my_pair ^ step, 2 * own_rows), z=step)
        rows = rows + part.astype(f32)
    mine = rows_of(rows, my_core, own_rows)
    other = swap(rows_of(rows, 1 - my_core, own_rows), core=1)
    block = by_core(my_core, mine, other)
    pieces = [block] + [swap(block, dp=step) for step in range(1, planes)]
    (update,) = call(
        functools.partial(update_kernel, planes, taps, out, 1.0 / math.sqrt(count)),
        (at_plane, inv_g, *pieces),
        [shape((taps * own_rows, channels), f32)],
        [pltpu.VMEM((taps * own_rows, channels), f32), pltpu.VMEM((channels, channels), f32)],
        6 * 2 * taps * own_rows * channels**2,
        scalars=1,
    )
    update = update.reshape(taps, own_rows, channels).transpose(1, 0, 2)

    last = results[1]
    last = swap(after(last, over_z), dp=planes - 1)
    mine = [*back[:-1], last]
    theirs = [*theirs[:-1], swap(last, core=1)]
    (activated,) = call(
        functools.partial(sort_kernel, planes, out),
        (at_plane, at_core, *mine, *theirs),
        [shape((channels, cells), bf16)],
        [],
        0,
        scalars=2,
    )
    return activated[None], update


def solution(mesh):
    planes = mesh.shape["dp"]
    pairs = mesh.shape["shard"] // 2
    return jax.shard_map(
        functools.partial(shards, planes, pairs),
        mesh=mesh,
        in_specs=(
            P(("dp", "shard"), None, None),
            P(("dp", "shard"), None, None),
            P("shard", None, None),
        ),
        out_specs=(P(("dp", "shard"), None, None), P("shard", None, None)),
        check_vma=False,
    )
```

```python
import functools
import math

import jax
import jax.numpy as jnp
import numpy as np
from jax import lax
from jax.experimental import pallas as pl
from jax.experimental.pallas import tpu as pltpu
from jax.sharding import PartitionSpec as P

SX = 4
SY = 16
SZ = 16
NS_ITERS = 8
DAMPING = 0.001
AXES = ("dp", "shard")
NT = (((1,), (1,)), ((), ()))
VMEM = pl.BlockSpec(memory_space=pltpu.VMEM)
ANY = pl.BlockSpec(memory_space=pl.ANY)
HBM = pl.BlockSpec(memory_space=pltpu.HBM)
SMEM = pl.BlockSpec(memory_space=pltpu.SMEM)
PARAMS = pltpu.CompilerParams(vmem_limit_bytes=32 * 1024 * 1024)


def exchange(x, planes, pairs, dp=0, z=0, core=0):
    perm = []
    for a in range(planes):
        for b in range(pairs):
            for c in range(2):
                here = (a * pairs + b) * 2 + c
                there = ((a ^ dp) * pairs + (b ^ z)) * 2 + (c ^ core)
                perm.append((here, there))
    return lax.ppermute(x, AXES, perm)


def after(x, *others):
    return lax.optimization_barrier((x, *others))[0]


def rows_of(x, index, height):
    return lax.dynamic_slice_in_dim(x, index * height, height, 0)


def place(buffer, block, index):
    return lax.dynamic_update_slice_in_dim(buffer, block, index * block.shape[0], 0)


def by_core(core, mine, other):
    return jnp.where(
        core == 0, jnp.concatenate([mine, other]), jnp.concatenate([other, mine])
    )


def dot3(left, right, dims=(((1,), (0,)), ((), ()))):
    left_high = left.astype(jnp.bfloat16)
    left_low = (left - left_high.astype(jnp.float32)).astype(jnp.bfloat16)
    right_high = right.astype(jnp.bfloat16)
    right_low = (right - right_high.astype(jnp.float32)).astype(jnp.bfloat16)

    def dot(a, b):
        return lax.dot_general(a, b, dims, preferred_element_type=jnp.float32)

    return dot(left_high, right_high) + (dot(left_high, right_low) + dot(left_low, right_high))


def shift_matrices():
    cell = np.arange(SY * SZ)
    parts = []
    for b in range(3):
        for c in range(3):
            meets_y = cell[:, None] // SZ + (b - 1) == cell[None, :] // SZ
            meets_z = cell[:, None] % SZ + (c - 1) == cell[None, :] % SZ
            parts.append(meets_y & meets_z)
    return jnp.asarray(np.concatenate(parts, axis=1), jnp.bfloat16)


def columns_kernel(pairs, out, at, *refs):
    blocks, (result, rows) = refs[:pairs], refs[pairs:]
    height = blocks[0].shape[0]
    channels = rows.shape[0]
    for step in range(pairs):
        start = pl.multiple_of((at[0] ^ step) * height, height)
        rows[pl.ds(start, height), :] = blocks[step][...].astype(jnp.float32)
    turned = rows[...].T.astype(jnp.bfloat16)
    for over in range(9):
        for c in range(3):
            tap = 3 * over + c
            result[over * out : (over + 1) * out, c * channels : (c + 1) * channels] = turned[
                tap * out : (tap + 1) * out, :
            ]


def slab(index):
    return slice(index * SY * SZ, (index + 1) * SY * SZ)


def forward_window(out, kernel, shifts, cot, stack, wide):
    channels, cells = stack.shape[0] // 3, stack.shape[1]
    for index in range(SX):
        middle = stack[channels : 2 * channels, slab(index)]
        for c, offset in ((0, 1), (2, 0)):
            stack[c * channels : (c + 1) * channels, slab(index)] = jnp.dot(
                middle, shifts[:, slab(offset)], preferred_element_type=jnp.float32
            ).astype(jnp.bfloat16)
    wide[...] = jnp.dot(kernel[...], stack[...], preferred_element_type=jnp.float32)
    along_y = lax.broadcasted_iota(jnp.int32, (out, cells), 1) // SZ % SY
    edge = jnp.zeros((out, SY * SZ), jnp.float32)
    outputs = None
    for a in range(3):
        first = 3 * a * out
        below = pltpu.roll(wide[first : first + out, :], SZ, 1)
        above = pltpu.roll(wide[first + 2 * out : first + 3 * out, :], cells - SZ, 1)
        part = (
            wide[first + out : first + 2 * out, :]
            + jnp.where(along_y > 0, below, 0.0)
            + jnp.where(along_y < SY - 1, above, 0.0)
        )
        if a == 0:
            part = jnp.concatenate([edge, part[:, : cells - SY * SZ]], axis=1)
        elif a == 2:
            part = jnp.concatenate([part[:, SY * SZ :], edge], axis=1)
        outputs = part if outputs is None else outputs + part
    sigma = jax.nn.sigmoid(outputs)
    activated = (outputs * sigma).astype(jnp.bfloat16)
    slope = cot.astype(jnp.float32) * sigma * (1.0 + outputs * (1.0 - sigma))
    return activated, slope.astype(jnp.bfloat16)


def gradient_windows(out, shifts, slopes, inputs, total_in, total, rows, moved):
    for window in range(2):
        for index in range(SX):
            start = (window * SX + index) * out
            rows[start : start + out, :] = slopes[
                window * out : (window + 1) * out, slab(index)
            ]
    for over in range(9):
        shifted = jnp.dot(
            rows[...], shifts[:, slab(over)], preferred_element_type=jnp.float32
        ).astype(jnp.bfloat16)
        for window in range(2):
            for index in range(SX):
                start = (window * SX + index) * out
                moved[window, over * out : (over + 1) * out, slab(index)] = shifted[
                    start : start + out, :
                ]
    height = 9 * out
    cells = moved.shape[2]
    near, far = slice(0, cells - SY * SZ), slice(SY * SZ, cells)
    spans = ((far, near), (slice(0, cells), slice(0, cells)), (near, far))
    for a, (of_slope, of_input) in enumerate(spans):
        sums = None
        for window in range(2):
            part = lax.dot_general(
                moved[window, :, of_slope],
                inputs[window][:, of_input],
                NT,
                preferred_element_type=jnp.float32,
            )
            sums = part if sums is None else sums + part
        at = slice(a * height, (a + 1) * height)
        total[at, :] = sums if total_in is None else total_in[at, :] + sums


def load(copies, semaphores):
    started = [
        pltpu.make_async_copy(source, target, semaphores.at[index])
        for index, (source, target) in enumerate(copies)
    ]
    for copy in started:
        copy.start()
    return started


def window_copies(pieces, inputs):
    copies = []
    start = 0
    for piece, height in pieces:
        copies.append((piece.at[pl.ds(0, height)], inputs.at[pl.ds(start, height)]))
        start += height
    return copies


def split(refs, heights):
    chips = []
    for parts in heights:
        count = len(parts)
        chips.append(
            (tuple(zip(refs[:count], parts)), tuple(zip(refs[count : 2 * count], parts)))
        )
        refs = refs[2 * count :]
    return chips, refs


def gather_window(pieces, inputs):
    start = 0
    for piece, height in pieces:
        inputs[start : start + height, :] = piece[:height, :]
        start += height


def forward_chip(out, core, kernel, for_z, windows, slopes, acts, stack, wide, gram):
    channels = stack.shape[0] // 3
    inputs = stack.at[channels : 2 * channels]
    half = channels // 2
    own = pl.multiple_of(core[0] * half, half)
    for window, pieces in enumerate(windows):
        gather_window(pieces, inputs)
        piece, height = pieces[0]
        first = pl.multiple_of(height + core[0] * out, out)
        at = slice(window * out, (window + 1) * out)
        acts[at, :], slopes[at, :] = forward_window(
            out, kernel, for_z, piece[pl.ds(first, out), :], stack, wide
        )
        part = lax.dot_general(
            inputs[pl.ds(own, half), :], inputs[...], NT, preferred_element_type=jnp.float32
        )
        gram = part if gram is None else gram + part
    return gram


def first_kernel(out, core, kernel, for_z, shifts, mine, theirs, *refs):
    stack, wide, held, semaphores, matrices, rows, moved = refs[-7:]
    refs = refs[:-7]
    chips = (len(refs) - 3) // 3
    payloads, (gram, total, *results) = refs[: 2 * chips], refs[2 * chips :]
    started = load(
        [(shifts, matrices), (mine, held.at[0]), (theirs, held.at[1])], semaphores
    )
    channels = gram.shape[1]
    sums = None
    windows = [payloads[2 * chip : 2 * chip + 2] for chip in range(chips)]
    for chip, pair in enumerate(windows + [(held.at[0], held.at[1])]):
        if chip == chips:
            for copy in started[1:]:
                copy.wait()
        result = results[(chip + 1) % (chips + 1)]
        pieces = tuple(((payload, channels),) for payload in pair)
        slopes, acts = result.at[: 2 * out], result.at[2 * out :]
        sums = forward_chip(out, core, kernel, for_z, pieces, slopes, acts, stack, wide, sums)
        if chip == 0:
            started[0].wait()
        inputs = tuple(payload.at[:channels] for payload in pair)
        gradient_windows(
            out, matrices, slopes, inputs, None if chip == 0 else total, total, rows, moved
        )
    gram[...] = sums


def last_kernel(out, heights, core, kernel, for_z, *refs):
    (windows,), (gram_in, gram, result, stack, wide) = split(refs, [heights])
    slopes, acts = result.at[: 2 * out], result.at[2 * out :]
    gram[...] = forward_chip(
        out, core, kernel, for_z, windows, slopes, acts, stack, wide, gram_in[...]
    )


def gradient_kernel(out, heights, shifts, slopes, total_in, *refs):
    (windows,), (total, inputs, rows, moved) = split(refs, [heights])
    for window, pieces in enumerate(windows):
        gather_window(pieces, inputs.at[window])
    gradient_windows(
        out, shifts, slopes, (inputs.at[0], inputs.at[1]), total_in, total, rows, moved
    )


def payload_kernel(planes, out, at, inputs, cotangent, *refs):
    payloads, (held, semaphores) = refs[:-2], refs[-2:]
    channels = inputs.shape[0]
    half = channels // 2
    for copy in load([(inputs, held.at[0]), (cotangent, held.at[1])], semaphores):
        copy.wait()
    for payload, steps in zip(payloads, payload_steps(planes)):
        payload[:channels, :] = held[0]
        start = channels
        for step in steps:
            for core in range(2):
                first = pl.multiple_of(core * half + (at[0] ^ step) * out, out)
                payload[start : start + out, :] = held[1, pl.ds(first, out), :]
                start += out


def payload_steps(planes):
    if planes == 4:
        return [(0,), (1, 3), (2,)]
    return [(step,) for step in range(planes)]


def halves_kernel(channels, split_at, first, second, low, high):
    low[:split_at, :] = first[:split_at, :]
    low[split_at:, :] = first[channels + low.shape[0] - split_at :, :]
    high[...] = second[split_at:channels, :]


def gram_kernel(planes, out, at, core, *refs):
    mine, theirs = refs[:planes], refs[planes : 2 * planes]
    result, slopes, semaphores = refs[2 * planes :]
    half = result.shape[0]
    cells = mine[0].shape[1]
    own = pl.multiple_of(core[0] * half, half)
    other = pl.multiple_of((1 - core[0]) * half, half)
    copies = []
    for step in range(planes):
        plane = (at[0] ^ step) * out
        for window in range(2):
            columns = pl.ds(window * cells, cells)
            for start, piece, rows in (
                (own, mine[step], window * out),
                (other, theirs[step], (1 - window) * out),
            ):
                target = pl.multiple_of(start + plane, out)
                copies.append(
                    (piece.at[pl.ds(rows, out)], slopes.at[pl.ds(target, out), columns])
                )
    for copy in load(copies, semaphores):
        copy.wait()
    result[...] = lax.dot_general(
        slopes[pl.ds(own, half), :], slopes[...], NT, preferred_element_type=jnp.float32
    )


def product_kernel(pairs, core, inverse, mine, theirs, result, narrow, rows):
    height = inverse.shape[0] // (2 * pairs)
    for pair in range(pairs):
        start = pl.multiple_of((2 * pair + core[0]) * height, height)
        rows[pair * height : (pair + 1) * height, :] = inverse[pl.ds(start, height), :]
    for index, gradient in ((core[0], mine), (1 - core[0], theirs)):
        product = dot3(rows[...], gradient[...], NT)
        result[index] = product
        narrow[index] = product.astype(jnp.bfloat16)


def sort_kernel(planes, out, at, core, *refs):
    mine, theirs = refs[:planes], refs[planes : 2 * planes]
    result, semaphores = refs[2 * planes :]
    half = result.shape[0] // 2
    copies = []
    for step in range(planes):
        plane = (at[0] ^ step) * out
        first = mine[step].shape[0] - 2 * out
        for start, piece, rows in (
            (core[0] * half, mine[step], first),
            ((1 - core[0]) * half, theirs[step], first + out),
        ):
            target = pl.multiple_of(start + plane, out)
            copies.append((piece.at[pl.ds(rows, out)], result.at[pl.ds(target, out)]))
    for copy in load(copies, semaphores):
        copy.wait()


def newton_kernel(count, core, mine, theirs, result, matrix, both):
    half, size = mine.shape
    matrix[pl.ds(pl.multiple_of(core[0] * half, half), half), :] = mine[...]
    matrix[pl.ds(pl.multiple_of((1 - core[0]) * half, half), half), :] = theirs[...]
    row = lax.broadcasted_iota(jnp.int32, (size, size), 0)
    column = lax.broadcasted_iota(jnp.int32, (size, size), 1)
    identity = jnp.where(row == column, 1.0, 0.0)
    factor = matrix[...] / count + DAMPING * identity
    diagonal = jnp.sum(factor * identity, axis=1, keepdims=True)
    scale = 1.0 / jnp.sum(diagonal, axis=0, keepdims=True)
    error = identity - factor * scale
    both[:size, :] = (identity + error) * scale
    both[size:, :] = error
    for sweep in range(1, NS_ITERS):
        if sweep == 1:
            both[size:, :] = dot3(error, error)
        last = sweep == NS_ITERS - 1
        products = dot3(both[:size, :] if last else both[...], both[size:, :])
        both[:size, :] += products[:size]
        if not last:
            both[size:, :] = products[size:]
    result[...] = both[:size, :]


def update_kernel(planes, taps, out, scale, at, inverse, *refs):
    pieces, (result, rows, factor) = refs[:planes], refs[planes:]
    own_rows = pieces[0].shape[1]
    half = inverse.shape[0] // 2
    for step in range(planes):
        for core in range(2):
            block = (step * 2 + core) * out
            start = pl.multiple_of(core * half + (at[0] ^ step) * out, out)
            factor[block : block + out, :] = inverse[pl.ds(start, out), :]
            for tap in range(taps):
                rows[tap * own_rows : (tap + 1) * own_rows, block : block + out] = pieces[step][
                    core, :, tap * out : (tap + 1) * out
                ]
    result[...] = dot3(rows[...], factor[...]) * scale


def call(kernel, args, shapes, scratch, flops, scalars=0, aliases=None, far=(), spec=ANY):
    moved = sum(a.size * a.dtype.itemsize for a in list(args) + list(shapes))
    in_specs = [SMEM] * scalars + [VMEM] * (len(args) - scalars)
    for index in far:
        in_specs[index] = spec
    return pl.pallas_call(
        kernel,
        out_shape=tuple(shapes),
        in_specs=in_specs,
        out_specs=tuple([VMEM] * len(shapes)),
        scratch_shapes=scratch,
        input_output_aliases=aliases or {},
        compiler_params=PARAMS,
        cost_estimate=pl.CostEstimate(flops=flops, bytes_accessed=moved, transcendentals=0),
    )(*args)


def shards(planes, pairs, activations, out_grad, weights):
    f32, bf16 = jnp.float32, jnp.bfloat16
    shape = jax.ShapeDtypeStruct
    inputs = activations[0]
    cotangent = out_grad[0]
    channels, cells = inputs.shape
    own_rows, taps, _ = weights.shape
    out = channels // (2 * planes)
    half = channels // 2
    wide = taps * out
    my_plane = lax.axis_index("dp")
    my_index = lax.axis_index("shard")
    my_pair = my_index // 2
    my_core = my_index % 2
    at_plane = my_plane.reshape(1)
    at_pair = my_pair.reshape(1)
    at_core = my_core.reshape(1)
    swap = functools.partial(exchange, planes=planes, pairs=pairs)

    def kernel_columns(core):
        start = core * half + my_plane * out
        part = lax.dynamic_slice_in_dim(weights, start, out, 2)
        return part.reshape(own_rows, wide)

    block = by_core(my_core, kernel_columns(my_core), swap(kernel_columns(1 - my_core), core=1))
    blocks = [block] + [swap(block, z=step) for step in range(1, pairs)]
    (kernel,) = call(
        functools.partial(columns_kernel, pairs, out),
        (at_pair, *blocks),
        [shape((9 * out, 3 * channels), bf16)],
        [pltpu.VMEM((channels, wide), f32)],
        0,
        scalars=1,
    )

    steps = payload_steps(planes)
    payloads = call(
        functools.partial(payload_kernel, planes, out),
        (at_plane, inputs, cotangent),
        [shape((channels + 2 * out * len(targets), cells), bf16) for targets in steps],
        [pltpu.VMEM((2, channels, cells), bf16), pltpu.SemaphoreType.DMA((2,))],
        0,
        scalars=1,
        far=(1, 2),
        spec=HBM,
    )
    own, *arrived = payloads[:1] + tuple(
        swap(payload, dp=step) for step, payload in enumerate(payloads) if step > 0
    )
    own, *arrived = lax.optimization_barrier((own, *arrived, *blocks))[: len(arrived) + 1]
    windows = [[own]] + [[part] for part in arrived]
    heights = [(channels,)] * len(windows)
    if len(windows) < planes:
        split_at = half - out
        low, high = call(
            functools.partial(halves_kernel, channels, split_at),
            arrived,
            [shape((half + out, cells), bf16)] * 2,
            [],
            0,
        )
        windows.append([swap(low, dp=2), swap(high, dp=1)])
        heights.append((split_at, channels - split_at))

    shifts = shift_matrices()
    half_flops = 2 * 2 * wide * channels * cells

    for_forward = [pltpu.VMEM((3 * channels, cells), bf16), pltpu.VMEM((9 * out, cells), f32)]
    for_gradient = [
        pltpu.VMEM((2 * SX * out, SY * SZ), bf16),
        pltpu.VMEM((2, 9 * out, cells), bf16),
    ]

    for_z = jnp.concatenate(
        [shifts[:, 3 * SY * SZ : 4 * SY * SZ], shifts[:, 5 * SY * SZ : 6 * SY * SZ]], axis=1
    )
    near = [part for ((mine,)) in windows[1:-1] for part in (mine, swap(mine, core=1))]
    a_half, total, *results = call(
        functools.partial(first_kernel, out),
        (at_core, kernel, for_z, shifts, own, swap(own, core=1), *near),
        [shape((half, channels), f32), shape((wide, channels), f32)]
        + [shape((4 * out, cells), bf16)] * (planes - 1),
        for_forward
        + [
            pltpu.VMEM((2, *own.shape), bf16),
            pltpu.SemaphoreType.DMA((3,)),
            pltpu.VMEM(shifts.shape, bf16),
        ]
        + for_gradient,
        2 * half_flops * (planes - 1),
        scalars=1,
        far=(3, 4, 5),
    )
    mine = [after(part, results[-1]) for part in windows[-1]]
    pieces = mine + [swap(part, core=1) for part in mine]
    a_half, result = call(
        functools.partial(last_kernel, out, heights[-1]),
        (at_core, kernel, for_z, *pieces, a_half),
        [shape((half, channels), f32), shape((4 * out, cells), bf16)],
        for_forward,
        half_flops,
        scalars=1,
    )
    (total,) = call(
        functools.partial(gradient_kernel, out, heights[-1]),
        (shifts, result, total, *pieces),
        [shape((wide, channels), f32)],
        [pltpu.VMEM((2, channels, cells), bf16)] + for_gradient,
        half_flops,
        aliases={2: 0},
    )
    back = [results[0]] + [
        swap(part, dp=step) for step, part in enumerate(results) if step > 0
    ]
    back = [after(part, result) for part in back] + [swap(result, dp=planes - 1)]
    theirs = [swap(result, core=1) for result in back]

    part = a_half
    for step in range(1, pairs):
        a_half = a_half + swap(part, z=step)
    a_half = after(a_half, total)

    count = planes * pairs * 2 * cells

    def inverse_of(mine):
        return call(
            functools.partial(newton_kernel, count),
            (at_core, mine, swap(mine, core=1)),
            [shape((channels, channels), f32)],
            [pltpu.VMEM((channels, channels), f32), pltpu.VMEM((2 * channels, channels), f32)],
            6 * NS_ITERS * 4 * channels**3,
            scalars=1,
        )[0]

    (g_half,) = call(
        functools.partial(gram_kernel, planes, out),
        (at_plane, at_core, *back, *theirs),
        [shape((half, channels), f32)],
        [pltpu.VMEM((channels, 2 * cells), bf16), pltpu.SemaphoreType.DMA((4 * planes,))],
        2 * 2 * half * channels * cells,
        scalars=2,
        far=range(2, 2 + 2 * planes),
    )
    inv_a = inverse_of(a_half)
    height = pairs * own_rows
    product, narrow = call(
        functools.partial(product_kernel, pairs),
        (at_core, inv_a, total, swap(total, core=1)),
        [shape((2, height, wide), f32), shape((2, height, wide), bf16)],
        [pltpu.VMEM((height, channels), f32)],
        3 * 2 * channels**2 * wide,
        scalars=1,
    )

    def part_for(array, pair):
        return lax.dynamic_slice_in_dim(array, pair * own_rows, own_rows, 1)

    block = part_for(product, my_pair)
    for step in range(1, pairs):
        block = block + swap(part_for(narrow, my_pair ^ step), z=step).astype(f32)
    g_half = after(g_half, a_half)
    part = rows_of(g_half, my_plane, out)
    for step in range(1, planes):
        part = part + swap(rows_of(g_half, my_plane ^ step, out), dp=step)
    part = after(part, inv_a)
    over_z = part
    for step in range(1, pairs):
        over_z = over_z + swap(part, z=step)
    over_z = after(over_z, narrow)
    g_half = jnp.zeros((half, channels), f32)
    for step in range(planes):
        part = over_z if step == 0 else swap(over_z, dp=step)
        g_half = place(g_half, part, my_plane ^ step)

    inv_g = inverse_of(g_half)

    pieces = [block] + [swap(block, dp=step) for step in range(1, planes)]
    (update,) = call(
        functools.partial(update_kernel, planes, taps, out, 1.0 / math.sqrt(count)),
        (at_plane, inv_g, *pieces),
        [shape((taps * own_rows, channels), f32)],
        [pltpu.VMEM((taps * own_rows, channels), f32), pltpu.VMEM((channels, channels), f32)],
        6 * 2 * taps * own_rows * channels**2,
        scalars=1,
    )
    update = update.reshape(taps, own_rows, channels).transpose(1, 0, 2)

    (activated,) = call(
        functools.partial(sort_kernel, planes, out),
        (at_plane, at_core, *back, *theirs),
        [shape((channels, cells), bf16)],
        [pltpu.SemaphoreType.DMA((2 * planes,))],
        0,
        scalars=2,
        far=range(2, 2 + 2 * planes),
    )
    return activated[None], update


def solution(mesh):
    planes = mesh.shape["dp"]
    pairs = mesh.shape["shard"] // 2
    return jax.shard_map(
        functools.partial(shards, planes, pairs),
        mesh=mesh,
        in_specs=(
            P(("dp", "shard"), None, None),
            P(("dp", "shard"), None, None),
            P("shard", None, None),
        ),
        out_specs=(P(("dp", "shard"), None, None), P("shard", None, None)),
        check_vma=False,
    )
```

```python
import functools
import math

import jax
import jax.numpy as jnp
import numpy as np
from jax import lax
from jax.experimental import pallas as pl
from jax.experimental.pallas import tpu as pltpu
from jax.sharding import PartitionSpec as P

SX = 4
SY = 16
SZ = 16
NS_ITERS = 8
DAMPING = 0.001
AXES = ("dp", "shard")
NT = (((1,), (1,)), ((), ()))
VMEM = pl.BlockSpec(memory_space=pltpu.VMEM)
ANY = pl.BlockSpec(memory_space=pl.ANY)
HBM = pl.BlockSpec(memory_space=pltpu.HBM)
SMEM = pl.BlockSpec(memory_space=pltpu.SMEM)
PARAMS = pltpu.CompilerParams(vmem_limit_bytes=32 * 1024 * 1024)


def exchange(x, planes, pairs, dp=0, z=0, core=0):
    perm = []
    for a in range(planes):
        for b in range(pairs):
            for c in range(2):
                here = (a * pairs + b) * 2 + c
                there = ((a ^ dp) * pairs + (b ^ z)) * 2 + (c ^ core)
                perm.append((here, there))
    return lax.ppermute(x, AXES, perm)


def after(x, *others):
    return lax.optimization_barrier((x, *others))[0]


def rows_of(x, index, height):
    return lax.dynamic_slice_in_dim(x, index * height, height, 0)


def place(buffer, block, index):
    return lax.dynamic_update_slice_in_dim(buffer, block, index * block.shape[0], 0)


def by_core(core, mine, other):
    return jnp.where(
        core == 0, jnp.concatenate([mine, other]), jnp.concatenate([other, mine])
    )


def dot3(left, right, dims=(((1,), (0,)), ((), ()))):
    left_high = left.astype(jnp.bfloat16)
    left_low = (left - left_high.astype(jnp.float32)).astype(jnp.bfloat16)
    right_high = right.astype(jnp.bfloat16)
    right_low = (right - right_high.astype(jnp.float32)).astype(jnp.bfloat16)

    (left_dim,), (right_dim,) = dims[0]
    return lax.dot_general(
        jnp.concatenate([left_high, left_low, left_high], axis=left_dim),
        jnp.concatenate([right_high, right_high, right_low], axis=right_dim),
        dims,
        preferred_element_type=jnp.float32,
    )


def shift_matrices():
    cell = np.arange(SY * SZ)
    parts = []
    for b in range(3):
        for c in range(3):
            meets_y = cell[:, None] // SZ + (b - 1) == cell[None, :] // SZ
            meets_z = cell[:, None] % SZ + (c - 1) == cell[None, :] % SZ
            parts.append(meets_y & meets_z)
    return jnp.asarray(np.concatenate(parts, axis=1), jnp.bfloat16)


def columns_kernel(pairs, out, at, *refs):
    blocks, (result, rows) = refs[:pairs], refs[pairs:]
    height = blocks[0].shape[0]
    channels = rows.shape[0]
    for step in range(pairs):
        start = pl.multiple_of((at[0] ^ step) * height, height)
        rows[pl.ds(start, height), :] = blocks[step][...].astype(jnp.float32)
    turned = rows[...].T.astype(jnp.bfloat16)
    for over in range(9):
        for c in range(3):
            tap = 3 * over + c
            result[over * out : (over + 1) * out, c * channels : (c + 1) * channels] = turned[
                tap * out : (tap + 1) * out, :
            ]


def slab(index):
    return slice(index * SY * SZ, (index + 1) * SY * SZ)


def forward_window(out, kernel, shifts, cot, stack, wide):
    channels, cells = stack.shape[0] // 3, stack.shape[1]
    for index in range(SX):
        middle = stack[channels : 2 * channels, slab(index)]
        for c, offset in ((0, 1), (2, 0)):
            stack[c * channels : (c + 1) * channels, slab(index)] = jnp.dot(
                middle, shifts[:, slab(offset)], preferred_element_type=jnp.float32
            ).astype(jnp.bfloat16)
    wide[...] = jnp.dot(kernel[...], stack[...], preferred_element_type=jnp.float32)
    along_y = lax.broadcasted_iota(jnp.int32, (out, cells), 1) // SZ % SY
    edge = jnp.zeros((out, SY * SZ), jnp.float32)
    outputs = None
    for a in range(3):
        first = 3 * a * out
        below = pltpu.roll(wide[first : first + out, :], SZ, 1)
        above = pltpu.roll(wide[first + 2 * out : first + 3 * out, :], cells - SZ, 1)
        part = (
            wide[first + out : first + 2 * out, :]
            + jnp.where(along_y > 0, below, 0.0)
            + jnp.where(along_y < SY - 1, above, 0.0)
        )
        if a == 0:
            part = jnp.concatenate([edge, part[:, : cells - SY * SZ]], axis=1)
        elif a == 2:
            part = jnp.concatenate([part[:, SY * SZ :], edge], axis=1)
        outputs = part if outputs is None else outputs + part
    sigma = jax.nn.sigmoid(outputs)
    activated = (outputs * sigma).astype(jnp.bfloat16)
    slope = cot.astype(jnp.float32) * sigma * (1.0 + outputs * (1.0 - sigma))
    return activated, slope.astype(jnp.bfloat16)


def gradient_windows(out, shifts, slopes, inputs, total_in, total, rows, moved):
    for window in range(2):
        for index in range(SX):
            start = (window * SX + index) * out
            rows[start : start + out, :] = slopes[
                window * out : (window + 1) * out, slab(index)
            ]
    for over in range(9):
        shifted = jnp.dot(
            rows[...], shifts[:, slab(over)], preferred_element_type=jnp.float32
        ).astype(jnp.bfloat16)
        for window in range(2):
            for index in range(SX):
                start = (window * SX + index) * out
                moved[window, over * out : (over + 1) * out, slab(index)] = shifted[
                    start : start + out, :
                ]
    height = 9 * out
    cells = moved.shape[2]
    near, far = slice(0, cells - SY * SZ), slice(SY * SZ, cells)
    spans = ((far, near), (slice(0, cells), slice(0, cells)), (near, far))
    for a, (of_slope, of_input) in enumerate(spans):
        sums = None
        for window in range(2):
            part = lax.dot_general(
                moved[window, :, of_slope],
                inputs[window][:, of_input],
                NT,
                preferred_element_type=jnp.float32,
            )
            sums = part if sums is None else sums + part
        at = slice(a * height, (a + 1) * height)
        total[at, :] = sums if total_in is None else total_in[at, :] + sums


def load(copies, semaphores):
    started = [
        pltpu.make_async_copy(source, target, semaphores.at[index])
        for index, (source, target) in enumerate(copies)
    ]
    for copy in started:
        copy.start()
    return started


def window_copies(pieces, inputs):
    copies = []
    start = 0
    for piece, height in pieces:
        copies.append((piece.at[pl.ds(0, height)], inputs.at[pl.ds(start, height)]))
        start += height
    return copies


def split(refs, heights):
    chips = []
    for parts in heights:
        count = len(parts)
        chips.append(
            (tuple(zip(refs[:count], parts)), tuple(zip(refs[count : 2 * count], parts)))
        )
        refs = refs[2 * count :]
    return chips, refs


def gather_window(pieces, inputs):
    start = 0
    for piece, height in pieces:
        inputs[start : start + height, :] = piece[:height, :]
        start += height


def forward_chip(out, core, kernel, for_z, windows, slopes, acts, stack, wide, gram):
    channels = stack.shape[0] // 3
    inputs = stack.at[channels : 2 * channels]
    half = channels // 2
    own = pl.multiple_of(core[0] * half, half)
    for window, pieces in enumerate(windows):
        gather_window(pieces, inputs)
        piece, height = pieces[0]
        first = pl.multiple_of(height + core[0] * out, out)
        at = slice(window * out, (window + 1) * out)
        acts[at, :], slopes[at, :] = forward_window(
            out, kernel, for_z, piece[pl.ds(first, out), :], stack, wide
        )
        part = lax.dot_general(
            inputs[pl.ds(own, half), :], inputs[...], NT, preferred_element_type=jnp.float32
        )
        gram = part if gram is None else gram + part
    return gram


def first_kernel(out, core, kernel, for_z, shifts, mine, theirs, *refs):
    stack, wide, held, semaphores, matrices, rows, moved = refs[-7:]
    refs = refs[:-7]
    chips = (len(refs) - 3) // 3
    payloads, (gram, total, *results) = refs[: 2 * chips], refs[2 * chips :]
    started = load(
        [(shifts, matrices), (mine, held.at[0]), (theirs, held.at[1])], semaphores
    )
    channels = gram.shape[1]
    sums = None
    windows = [payloads[2 * chip : 2 * chip + 2] for chip in range(chips)]
    for chip, pair in enumerate(windows + [(held.at[0], held.at[1])]):
        if chip == chips:
            for copy in started[1:]:
                copy.wait()
        result = results[(chip + 1) % (chips + 1)]
        pieces = tuple(((payload, channels),) for payload in pair)
        slopes, acts = result.at[: 2 * out], result.at[2 * out :]
        sums = forward_chip(out, core, kernel, for_z, pieces, slopes, acts, stack, wide, sums)
        if chip == 0:
            started[0].wait()
        inputs = tuple(payload.at[:channels] for payload in pair)
        gradient_windows(
            out, matrices, slopes, inputs, None if chip == 0 else total, total, rows, moved
        )
    gram[...] = sums


def last_kernel(out, heights, core, kernel, for_z, *refs):
    (windows,), (gram_in, gram, result, stack, wide) = split(refs, [heights])
    slopes, acts = result.at[: 2 * out], result.at[2 * out :]
    gram[...] = forward_chip(
        out, core, kernel, for_z, windows, slopes, acts, stack, wide, gram_in[...]
    )


def gradient_kernel(out, heights, shifts, slopes, total_in, *refs):
    (windows,), (total, inputs, rows, moved) = split(refs, [heights])
    for window, pieces in enumerate(windows):
        gather_window(pieces, inputs.at[window])
    gradient_windows(
        out, shifts, slopes, (inputs.at[0], inputs.at[1]), total_in, total, rows, moved
    )


def payload_kernel(planes, out, at, inputs, cotangent, *refs):
    payloads, (held, semaphores) = refs[:-2], refs[-2:]
    channels = inputs.shape[0]
    half = channels // 2
    for copy in load([(inputs, held.at[0]), (cotangent, held.at[1])], semaphores):
        copy.wait()
    for payload, steps in zip(payloads, payload_steps(planes)):
        payload[:channels, :] = held[0]
        start = channels
        for step in steps:
            for core in range(2):
                first = pl.multiple_of(core * half + (at[0] ^ step) * out, out)
                payload[start : start + out, :] = held[1, pl.ds(first, out), :]
                start += out


def payload_steps(planes):
    if planes == 4:
        return [(0,), (1, 3), (2,)]
    return [(step,) for step in range(planes)]


def halves_kernel(channels, split_at, first, second, low, high):
    low[:split_at, :] = first[:split_at, :]
    low[split_at:, :] = first[channels + low.shape[0] - split_at :, :]
    high[...] = second[split_at:channels, :]


def gram_kernel(planes, out, at, core, *refs):
    mine, theirs = refs[:planes], refs[planes : 2 * planes]
    result, slopes, semaphores = refs[2 * planes :]
    half = result.shape[0]
    cells = mine[0].shape[1]
    own = pl.multiple_of(core[0] * half, half)
    other = pl.multiple_of((1 - core[0]) * half, half)
    copies = []
    for step in range(planes):
        plane = (at[0] ^ step) * out
        for window in range(2):
            columns = pl.ds(window * cells, cells)
            for start, piece, rows in (
                (own, mine[step], window * out),
                (other, theirs[step], (1 - window) * out),
            ):
                target = pl.multiple_of(start + plane, out)
                copies.append(
                    (piece.at[pl.ds(rows, out)], slopes.at[pl.ds(target, out), columns])
                )
    for copy in load(copies, semaphores):
        copy.wait()
    result[...] = lax.dot_general(
        slopes[pl.ds(own, half), :], slopes[...], NT, preferred_element_type=jnp.float32
    )


def product_kernel(pairs, core, inverse, mine, theirs, result, narrow, rows):
    height = inverse.shape[0] // (2 * pairs)
    for pair in range(pairs):
        start = pl.multiple_of((2 * pair + core[0]) * height, height)
        rows[pair * height : (pair + 1) * height, :] = inverse[pl.ds(start, height), :]
    for index, gradient in ((core[0], mine), (1 - core[0], theirs)):
        product = dot3(rows[...], gradient[...], NT)
        result[index] = product
        narrow[index] = product.astype(jnp.bfloat16)


def sort_kernel(planes, out, at, core, *refs):
    mine, theirs = refs[:planes], refs[planes : 2 * planes]
    result, semaphores = refs[2 * planes :]
    half = result.shape[0] // 2
    copies = []
    for step in range(planes):
        plane = (at[0] ^ step) * out
        first = mine[step].shape[0] - 2 * out
        for start, piece, rows in (
            (core[0] * half, mine[step], first),
            ((1 - core[0]) * half, theirs[step], first + out),
        ):
            target = pl.multiple_of(start + plane, out)
            copies.append((piece.at[pl.ds(rows, out)], result.at[pl.ds(target, out)]))
    for copy in load(copies, semaphores):
        copy.wait()


def newton_kernel(count, core, mine, theirs, result, matrix, both):
    half, size = mine.shape
    matrix[pl.ds(pl.multiple_of(core[0] * half, half), half), :] = mine[...]
    matrix[pl.ds(pl.multiple_of((1 - core[0]) * half, half), half), :] = theirs[...]
    row = lax.broadcasted_iota(jnp.int32, (size, size), 0)
    column = lax.broadcasted_iota(jnp.int32, (size, size), 1)
    identity = jnp.where(row == column, 1.0, 0.0)
    factor = matrix[...] / count + DAMPING * identity
    diagonal = jnp.sum(factor * identity, axis=1, keepdims=True)
    scale = 1.0 / jnp.sum(diagonal, axis=0, keepdims=True)
    error = identity - factor * scale
    both[:size, :] = (identity + error) * scale
    both[size:, :] = error
    for sweep in range(1, NS_ITERS):
        if sweep == 1:
            both[size:, :] = dot3(error, error)
        last = sweep == NS_ITERS - 1
        products = dot3(both[:size, :] if last else both[...], both[size:, :])
        both[:size, :] += products[:size]
        if not last:
            both[size:, :] = products[size:]
    result[...] = both[:size, :]


def update_kernel(planes, taps, out, scale, at, inverse, *refs):
    pieces, (result, rows, factor) = refs[:planes], refs[planes:]
    own_rows = pieces[0].shape[1]
    half = inverse.shape[0] // 2
    for step in range(planes):
        for core in range(2):
            block = (step * 2 + core) * out
            start = pl.multiple_of(core * half + (at[0] ^ step) * out, out)
            factor[block : block + out, :] = inverse[pl.ds(start, out), :]
            for tap in range(taps):
                rows[tap * own_rows : (tap + 1) * own_rows, block : block + out] = pieces[step][
                    core, :, tap * out : (tap + 1) * out
                ].astype(jnp.float32)
    result[...] = dot3(rows[...], factor[...]) * scale


def call(kernel, args, shapes, scratch, flops, scalars=0, aliases=None, far=(), spec=ANY):
    moved = sum(a.size * a.dtype.itemsize for a in list(args) + list(shapes))
    in_specs = [SMEM] * scalars + [VMEM] * (len(args) - scalars)
    for index in far:
        in_specs[index] = spec
    return pl.pallas_call(
        kernel,
        out_shape=tuple(shapes),
        in_specs=in_specs,
        out_specs=tuple([VMEM] * len(shapes)),
        scratch_shapes=scratch,
        input_output_aliases=aliases or {},
        compiler_params=PARAMS,
        cost_estimate=pl.CostEstimate(flops=flops, bytes_accessed=moved, transcendentals=0),
    )(*args)


def shards(planes, pairs, activations, out_grad, weights):
    f32, bf16 = jnp.float32, jnp.bfloat16
    shape = jax.ShapeDtypeStruct
    inputs = activations[0]
    cotangent = out_grad[0]
    channels, cells = inputs.shape
    own_rows, taps, _ = weights.shape
    out = channels // (2 * planes)
    half = channels // 2
    wide = taps * out
    my_plane = lax.axis_index("dp")
    my_index = lax.axis_index("shard")
    my_pair = my_index // 2
    my_core = my_index % 2
    at_plane = my_plane.reshape(1)
    at_pair = my_pair.reshape(1)
    at_core = my_core.reshape(1)
    swap = functools.partial(exchange, planes=planes, pairs=pairs)

    def kernel_columns(core):
        start = core * half + my_plane * out
        part = lax.dynamic_slice_in_dim(weights, start, out, 2)
        return part.reshape(own_rows, wide)

    block = by_core(my_core, kernel_columns(my_core), swap(kernel_columns(1 - my_core), core=1))
    blocks = [block] + [swap(block, z=step) for step in range(1, pairs)]
    (kernel,) = call(
        functools.partial(columns_kernel, pairs, out),
        (at_pair, *blocks),
        [shape((9 * out, 3 * channels), bf16)],
        [pltpu.VMEM((channels, wide), f32)],
        0,
        scalars=1,
    )

    steps = payload_steps(planes)
    payloads = call(
        functools.partial(payload_kernel, planes, out),
        (at_plane, inputs, cotangent),
        [shape((channels + 2 * out * len(targets), cells), bf16) for targets in steps],
        [pltpu.VMEM((2, channels, cells), bf16), pltpu.SemaphoreType.DMA((2,))],
        0,
        scalars=1,
        far=(1, 2),
        spec=HBM,
    )
    own, *arrived = payloads[:1] + tuple(
        swap(payload, dp=step) for step, payload in enumerate(payloads) if step > 0
    )
    own, *arrived = lax.optimization_barrier((own, *arrived, *blocks))[: len(arrived) + 1]
    windows = [[own]] + [[part] for part in arrived]
    heights = [(channels,)] * len(windows)
    if len(windows) < planes:
        split_at = half - out
        low, high = call(
            functools.partial(halves_kernel, channels, split_at),
            arrived,
            [shape((half + out, cells), bf16)] * 2,
            [],
            0,
        )
        windows.append([swap(low, dp=2), swap(high, dp=1)])
        heights.append((split_at, channels - split_at))

    shifts = shift_matrices()
    half_flops = 2 * 2 * wide * channels * cells

    for_forward = [pltpu.VMEM((3 * channels, cells), bf16), pltpu.VMEM((9 * out, cells), f32)]
    for_gradient = [
        pltpu.VMEM((2 * SX * out, SY * SZ), bf16),
        pltpu.VMEM((2, 9 * out, cells), bf16),
    ]

    for_z = jnp.concatenate(
        [shifts[:, 3 * SY * SZ : 4 * SY * SZ], shifts[:, 5 * SY * SZ : 6 * SY * SZ]], axis=1
    )
    near = [part for ((mine,)) in windows[1:-1] for part in (mine, swap(mine, core=1))]
    a_half, total, *results = call(
        functools.partial(first_kernel, out),
        (at_core, kernel, for_z, shifts, own, swap(own, core=1), *near),
        [shape((half, channels), f32), shape((wide, channels), f32)]
        + [shape((4 * out, cells), bf16)] * (planes - 1),
        for_forward
        + [
            pltpu.VMEM((2, *own.shape), bf16),
            pltpu.SemaphoreType.DMA((3,)),
            pltpu.VMEM(shifts.shape, bf16),
        ]
        + for_gradient,
        2 * half_flops * (planes - 1),
        scalars=1,
        far=(3, 4, 5),
    )
    mine = [after(part, results[-1]) for part in windows[-1]]
    pieces = mine + [swap(part, core=1) for part in mine]
    a_half, result = call(
        functools.partial(last_kernel, out, heights[-1]),
        (at_core, kernel, for_z, *pieces, a_half),
        [shape((half, channels), f32), shape((4 * out, cells), bf16)],
        for_forward,
        half_flops,
        scalars=1,
    )
    (total,) = call(
        functools.partial(gradient_kernel, out, heights[-1]),
        (shifts, result, total, *pieces),
        [shape((wide, channels), f32)],
        [pltpu.VMEM((2, channels, cells), bf16)] + for_gradient,
        half_flops,
        aliases={2: 0},
    )
    back = [results[0]] + [
        swap(part, dp=step) for step, part in enumerate(results) if step > 0
    ]
    back = [after(part, result) for part in back] + [swap(result, dp=planes - 1)]
    theirs = [swap(after(part, total), core=1) for part in back]

    part = a_half
    for step in range(1, pairs):
        a_half = a_half + swap(part, z=step)
    a_half = after(a_half, total)

    count = planes * pairs * 2 * cells

    def inverse_of(mine):
        return call(
            functools.partial(newton_kernel, count),
            (at_core, mine, swap(mine, core=1)),
            [shape((channels, channels), f32)],
            [pltpu.VMEM((channels, channels), f32), pltpu.VMEM((2 * channels, channels), f32)],
            6 * NS_ITERS * 4 * channels**3,
            scalars=1,
        )[0]

    (g_half,) = call(
        functools.partial(gram_kernel, planes, out),
        (at_plane, at_core, *back, *theirs),
        [shape((half, channels), f32)],
        [pltpu.VMEM((channels, 2 * cells), bf16), pltpu.SemaphoreType.DMA((4 * planes,))],
        2 * 2 * half * channels * cells,
        scalars=2,
        far=range(2, 2 + 2 * planes),
    )
    inv_a = inverse_of(a_half)
    height = pairs * own_rows
    product, narrow = call(
        functools.partial(product_kernel, pairs),
        (at_core, inv_a, total, swap(total, core=1)),
        [shape((2, height, wide), f32), shape((2, height, wide), bf16)],
        [pltpu.VMEM((height, channels), f32)],
        3 * 2 * channels**2 * wide,
        scalars=1,
    )

    def part_for(array, pair):
        return lax.dynamic_slice_in_dim(array, pair * own_rows, own_rows, 1)

    block = part_for(product, my_pair)
    for step in range(1, pairs):
        block = block + swap(part_for(narrow, my_pair ^ step), z=step).astype(f32)
    g_half = after(g_half, a_half)
    part = rows_of(g_half, my_plane, out)
    for step in range(1, planes):
        part = part + swap(rows_of(g_half, my_plane ^ step, out), dp=step)
    part = after(part, inv_a)
    over_z = part
    for step in range(1, pairs):
        over_z = over_z + swap(part, z=step)
    over_z = after(over_z, narrow)
    g_half = jnp.zeros((half, channels), f32)
    for step in range(planes):
        part = over_z if step == 0 else swap(over_z, dp=step)
        g_half = place(g_half, part, my_plane ^ step)

    inv_g = inverse_of(g_half)

    block = block.astype(bf16)
    pieces = [block] + [swap(block, dp=step) for step in range(1, planes)]
    (update,) = call(
        functools.partial(update_kernel, planes, taps, out, 1.0 / math.sqrt(count)),
        (at_plane, inv_g, *pieces),
        [shape((taps * own_rows, channels), f32)],
        [pltpu.VMEM((taps * own_rows, channels), f32), pltpu.VMEM((channels, channels), f32)],
        6 * 2 * taps * own_rows * channels**2,
        scalars=1,
    )
    update = update.reshape(taps, own_rows, channels).transpose(1, 0, 2)

    (activated,) = call(
        functools.partial(sort_kernel, planes, out),
        (at_plane, at_core, *back, *theirs),
        [shape((channels, cells), bf16)],
        [pltpu.SemaphoreType.DMA((2 * planes,))],
        0,
        scalars=2,
        far=range(2, 2 + 2 * planes),
    )
    return activated[None], update


def solution(mesh):
    planes = mesh.shape["dp"]
    pairs = mesh.shape["shard"] // 2
    return jax.shard_map(
        functools.partial(shards, planes, pairs),
        mesh=mesh,
        in_specs=(
            P(("dp", "shard"), None, None),
            P(("dp", "shard"), None, None),
            P("shard", None, None),
        ),
        out_specs=(P(("dp", "shard"), None, None), P("shard", None, None)),
        check_vma=False,
    )
```

```python
import functools
import math

import jax
import jax.numpy as jnp
import numpy as np
from jax import lax
from jax.experimental import pallas as pl
from jax.experimental.pallas import tpu as pltpu
from jax.sharding import PartitionSpec as P

SX = 4
SY = 16
SZ = 16
NS_ITERS = 8
DAMPING = 0.001
AXES = ("dp", "shard")
NT = (((1,), (1,)), ((), ()))
VMEM = pl.BlockSpec(memory_space=pltpu.VMEM)
ANY = pl.BlockSpec(memory_space=pl.ANY)
HBM = pl.BlockSpec(memory_space=pltpu.HBM)
SMEM = pl.BlockSpec(memory_space=pltpu.SMEM)
PARAMS = pltpu.CompilerParams(vmem_limit_bytes=32 * 1024 * 1024)


def exchange(x, planes, pairs, dp=0, z=0, core=0):
    perm = []
    for a in range(planes):
        for b in range(pairs):
            for c in range(2):
                here = (a * pairs + b) * 2 + c
                there = ((a ^ dp) * pairs + (b ^ z)) * 2 + (c ^ core)
                perm.append((here, there))
    return lax.ppermute(x, AXES, perm)


def after(x, *others):
    return lax.optimization_barrier((x, *others))[0]


def rows_of(x, index, height):
    return lax.dynamic_slice_in_dim(x, index * height, height, 0)


def place(buffer, block, index):
    return lax.dynamic_update_slice_in_dim(buffer, block, index * block.shape[0], 0)


def by_core(core, mine, other):
    return jnp.where(
        core == 0, jnp.concatenate([mine, other]), jnp.concatenate([other, mine])
    )


def dot3(left, right, dims=(((1,), (0,)), ((), ()))):
    left_high = left.astype(jnp.bfloat16)
    left_low = (left - left_high.astype(jnp.float32)).astype(jnp.bfloat16)
    right_high = right.astype(jnp.bfloat16)
    right_low = (right - right_high.astype(jnp.float32)).astype(jnp.bfloat16)

    (left_dim,), (right_dim,) = dims[0]
    return lax.dot_general(
        jnp.concatenate([left_high, left_low, left_high], axis=left_dim),
        jnp.concatenate([right_high, right_high, right_low], axis=right_dim),
        dims,
        preferred_element_type=jnp.float32,
    )


def shift_matrices():
    cell = np.arange(SY * SZ)
    parts = []
    for b in range(3):
        for c in range(3):
            meets_y = cell[:, None] // SZ + (b - 1) == cell[None, :] // SZ
            meets_z = cell[:, None] % SZ + (c - 1) == cell[None, :] % SZ
            parts.append(meets_y & meets_z)
    return jnp.asarray(np.concatenate(parts, axis=1), jnp.bfloat16)


def columns_kernel(pairs, out, at, *refs):
    blocks, (result, rows) = refs[:pairs], refs[pairs:]
    height = blocks[0].shape[0]
    channels = rows.shape[0]
    for step in range(pairs):
        start = pl.multiple_of((at[0] ^ step) * height, height)
        rows[pl.ds(start, height), :] = blocks[step][...].astype(jnp.float32)
    turned = rows[...].T.astype(jnp.bfloat16)
    for over in range(9):
        for c in range(3):
            tap = 3 * over + c
            result[over * out : (over + 1) * out, c * channels : (c + 1) * channels] = turned[
                tap * out : (tap + 1) * out, :
            ]


def slab(index):
    return slice(index * SY * SZ, (index + 1) * SY * SZ)


def forward_window(out, kernel, shifts, cot, stack, wide):
    channels, cells = stack.shape[0] // 3, stack.shape[1]
    for index in range(SX):
        middle = stack[channels : 2 * channels, slab(index)]
        for c, offset in ((0, 1), (2, 0)):
            stack[c * channels : (c + 1) * channels, slab(index)] = jnp.dot(
                middle, shifts[:, slab(offset)], preferred_element_type=jnp.float32
            ).astype(jnp.bfloat16)
    wide[...] = jnp.dot(kernel[...], stack[...], preferred_element_type=jnp.float32)
    along_y = lax.broadcasted_iota(jnp.int32, (out, cells), 1) // SZ % SY
    edge = jnp.zeros((out, SY * SZ), jnp.float32)
    outputs = None
    for a in range(3):
        first = 3 * a * out
        below = pltpu.roll(wide[first : first + out, :], SZ, 1)
        above = pltpu.roll(wide[first + 2 * out : first + 3 * out, :], cells - SZ, 1)
        part = (
            wide[first + out : first + 2 * out, :]
            + jnp.where(along_y > 0, below, 0.0)
            + jnp.where(along_y < SY - 1, above, 0.0)
        )
        if a == 0:
            part = jnp.concatenate([edge, part[:, : cells - SY * SZ]], axis=1)
        elif a == 2:
            part = jnp.concatenate([part[:, SY * SZ :], edge], axis=1)
        outputs = part if outputs is None else outputs + part
    sigma = jax.nn.sigmoid(outputs)
    activated = (outputs * sigma).astype(jnp.bfloat16)
    slope = cot.astype(jnp.float32) * sigma * (1.0 + outputs * (1.0 - sigma))
    return activated, slope.astype(jnp.bfloat16)


def gradient_windows(out, shifts, slopes, inputs, total_in, total, rows, moved):
    for window in range(2):
        for index in range(SX):
            start = (window * SX + index) * out
            rows[start : start + out, :] = slopes[
                window * out : (window + 1) * out, slab(index)
            ]
    for over in range(9):
        shifted = jnp.dot(
            rows[...], shifts[:, slab(over)], preferred_element_type=jnp.float32
        ).astype(jnp.bfloat16)
        for window in range(2):
            for index in range(SX):
                start = (window * SX + index) * out
                moved[window, over * out : (over + 1) * out, slab(index)] = shifted[
                    start : start + out, :
                ]
    height = 9 * out
    cells = moved.shape[2]
    near, far = slice(0, cells - SY * SZ), slice(SY * SZ, cells)
    spans = ((far, near), (slice(0, cells), slice(0, cells)), (near, far))
    for a, (of_slope, of_input) in enumerate(spans):
        sums = None
        for window in range(2):
            part = lax.dot_general(
                moved[window, :, of_slope],
                inputs[window][:, of_input],
                NT,
                preferred_element_type=jnp.float32,
            )
            sums = part if sums is None else sums + part
        at = slice(a * height, (a + 1) * height)
        total[at, :] = sums if total_in is None else total_in[at, :] + sums


def load(copies, semaphores):
    started = [
        pltpu.make_async_copy(source, target, semaphores.at[index])
        for index, (source, target) in enumerate(copies)
    ]
    for copy in started:
        copy.start()
    return started


def window_copies(pieces, inputs):
    copies = []
    start = 0
    for piece, height in pieces:
        copies.append((piece.at[pl.ds(0, height)], inputs.at[pl.ds(start, height)]))
        start += height
    return copies


def split(refs, heights):
    chips = []
    for parts in heights:
        count = len(parts)
        chips.append(
            (tuple(zip(refs[:count], parts)), tuple(zip(refs[count : 2 * count], parts)))
        )
        refs = refs[2 * count :]
    return chips, refs


def gather_window(pieces, inputs):
    start = 0
    for piece, height in pieces:
        inputs[start : start + height, :] = piece[:height, :]
        start += height


def forward_chip(out, core, kernel, for_z, windows, slopes, acts, stack, wide, gram):
    channels = stack.shape[0] // 3
    inputs = stack.at[channels : 2 * channels]
    half = channels // 2
    own = pl.multiple_of(core[0] * half, half)
    for window, pieces in enumerate(windows):
        gather_window(pieces, inputs)
        piece, height = pieces[0]
        first = pl.multiple_of(height + core[0] * out, out)
        at = slice(window * out, (window + 1) * out)
        acts[at, :], slopes[at, :] = forward_window(
            out, kernel, for_z, piece[pl.ds(first, out), :], stack, wide
        )
        part = lax.dot_general(
            inputs[pl.ds(own, half), :], inputs[...], NT, preferred_element_type=jnp.float32
        )
        gram = part if gram is None else gram + part
    return gram


def first_kernel(out, core, kernel, for_z, shifts, mine, theirs, *refs):
    stack, wide, held, semaphores, matrices, rows, moved = refs[-7:]
    refs = refs[:-7]
    chips = (len(refs) - 3) // 3
    payloads, (gram, total, *results) = refs[: 2 * chips], refs[2 * chips :]
    started = load(
        [(shifts, matrices), (mine, held.at[0]), (theirs, held.at[1])], semaphores
    )
    channels = gram.shape[1]
    sums = None
    windows = [payloads[2 * chip : 2 * chip + 2] for chip in range(chips)]
    for chip, pair in enumerate(windows + [(held.at[0], held.at[1])]):
        if chip == chips:
            for copy in started[1:]:
                copy.wait()
        result = results[(chip + 1) % (chips + 1)]
        pieces = tuple(((payload, channels),) for payload in pair)
        slopes, acts = result.at[: 2 * out], result.at[2 * out :]
        sums = forward_chip(out, core, kernel, for_z, pieces, slopes, acts, stack, wide, sums)
        if chip == 0:
            started[0].wait()
        inputs = tuple(payload.at[:channels] for payload in pair)
        gradient_windows(
            out, matrices, slopes, inputs, None if chip == 0 else total, total, rows, moved
        )
    gram[...] = sums


def last_kernel(out, heights, core, kernel, for_z, *refs):
    (windows,), (gram_in, gram, result, stack, wide) = split(refs, [heights])
    slopes, acts = result.at[: 2 * out], result.at[2 * out :]
    gram[...] = forward_chip(
        out, core, kernel, for_z, windows, slopes, acts, stack, wide, gram_in[...]
    )


def gradient_kernel(out, heights, shifts, slopes, total_in, *refs):
    (windows,), (total, inputs, rows, moved) = split(refs, [heights])
    for window, pieces in enumerate(windows):
        gather_window(pieces, inputs.at[window])
    gradient_windows(
        out, shifts, slopes, (inputs.at[0], inputs.at[1]), total_in, total, rows, moved
    )


def payload_kernel(planes, out, at, inputs, cotangent, *refs):
    payloads, (held, semaphores) = refs[:-2], refs[-2:]
    channels = inputs.shape[0]
    half = channels // 2
    for copy in load([(inputs, held.at[0]), (cotangent, held.at[1])], semaphores):
        copy.wait()
    for payload, steps in zip(payloads, payload_steps(planes)):
        payload[:channels, :] = held[0]
        start = channels
        for step in steps:
            for core in range(2):
                first = pl.multiple_of(core * half + (at[0] ^ step) * out, out)
                payload[start : start + out, :] = held[1, pl.ds(first, out), :]
                start += out


def payload_steps(planes):
    if planes == 4:
        return [(0,), (1, 3), (2,)]
    return [(step,) for step in range(planes)]


def halves_kernel(channels, split_at, first, second, low, high):
    low[:split_at, :] = first[:split_at, :]
    low[split_at:, :] = first[channels + low.shape[0] - split_at :, :]
    high[...] = second[split_at:channels, :]


def gram_kernel(planes, out, at, core, *refs):
    mine, theirs = refs[:planes], refs[planes : 2 * planes]
    result, slopes, semaphores = refs[2 * planes :]
    half = result.shape[0]
    cells = mine[0].shape[1]
    own = pl.multiple_of(core[0] * half, half)
    other = pl.multiple_of((1 - core[0]) * half, half)
    copies = []
    for step in range(planes):
        plane = (at[0] ^ step) * out
        for window in range(2):
            columns = pl.ds(window * cells, cells)
            for start, piece, rows in (
                (own, mine[step], window * out),
                (other, theirs[step], (1 - window) * out),
            ):
                target = pl.multiple_of(start + plane, out)
                copies.append(
                    (piece.at[pl.ds(rows, out)], slopes.at[pl.ds(target, out), columns])
                )
    for copy in load(copies, semaphores):
        copy.wait()
    result[...] = lax.dot_general(
        slopes[pl.ds(own, half), :], slopes[...], NT, preferred_element_type=jnp.float32
    )


def product_kernel(pairs, core, inverse, mine, theirs, result, narrow, rows):
    height = inverse.shape[0] // (2 * pairs)
    for pair in range(pairs):
        start = pl.multiple_of((2 * pair + core[0]) * height, height)
        rows[pair * height : (pair + 1) * height, :] = inverse[pl.ds(start, height), :]
    for index, gradient in ((core[0], mine), (1 - core[0], theirs)):
        product = dot3(rows[...], gradient[...], NT)
        result[index] = product
        narrow[index] = product.astype(jnp.bfloat16)


def sort_kernel(planes, out, at, core, *refs):
    mine, theirs = refs[:planes], refs[planes : 2 * planes]
    result, semaphores = refs[2 * planes :]
    half = result.shape[0] // 2
    copies = []
    for step in range(planes):
        plane = (at[0] ^ step) * out
        first = mine[step].shape[0] - 2 * out
        for start, piece, rows in (
            (core[0] * half, mine[step], first),
            ((1 - core[0]) * half, theirs[step], first + out),
        ):
            target = pl.multiple_of(start + plane, out)
            copies.append((piece.at[pl.ds(rows, out)], result.at[pl.ds(target, out)]))
    for copy in load(copies, semaphores):
        copy.wait()


def newton_kernel(count, core, mine, theirs, result, matrix, both):
    half, size = mine.shape
    matrix[pl.ds(pl.multiple_of(core[0] * half, half), half), :] = mine[...]
    matrix[pl.ds(pl.multiple_of((1 - core[0]) * half, half), half), :] = theirs[...]
    row = lax.broadcasted_iota(jnp.int32, (size, size), 0)
    column = lax.broadcasted_iota(jnp.int32, (size, size), 1)
    identity = jnp.where(row == column, 1.0, 0.0)
    factor = matrix[...] / count + DAMPING * identity
    diagonal = jnp.sum(factor * identity, axis=1, keepdims=True)
    scale = 1.0 / jnp.sum(diagonal, axis=0, keepdims=True)
    error = identity - factor * scale
    both[:size, :] = (identity + error) * scale
    both[size:, :] = error
    for sweep in range(1, NS_ITERS):
        if sweep == 1:
            both[size:, :] = dot3(error, error)
        last = sweep == NS_ITERS - 1
        products = dot3(both[:size, :] if last else both[...], both[size:, :])
        both[:size, :] += products[:size]
        if not last:
            both[size:, :] = products[size:]
    result[...] = both[:size, :]


def update_kernel(planes, taps, out, scale, at, inverse, *refs):
    pieces, (result, rows, factor) = refs[:planes], refs[planes:]
    own_rows = pieces[0].shape[1]
    half = inverse.shape[0] // 2
    for step in range(planes):
        for core in range(2):
            block = (step * 2 + core) * out
            start = pl.multiple_of(core * half + (at[0] ^ step) * out, out)
            factor[block : block + out, :] = inverse[pl.ds(start, out), :]
            for tap in range(taps):
                rows[tap * own_rows : (tap + 1) * own_rows, block : block + out] = pieces[step][
                    core, :, tap * out : (tap + 1) * out
                ].astype(jnp.float32)
    result[...] = dot3(rows[...], factor[...]) * scale


def call(kernel, args, shapes, scratch, flops, scalars=0, aliases=None, far=(), spec=ANY):
    moved = sum(a.size * a.dtype.itemsize for a in list(args) + list(shapes))
    in_specs = [SMEM] * scalars + [VMEM] * (len(args) - scalars)
    for index in far:
        in_specs[index] = spec
    return pl.pallas_call(
        kernel,
        out_shape=tuple(shapes),
        in_specs=in_specs,
        out_specs=tuple([VMEM] * len(shapes)),
        scratch_shapes=scratch,
        input_output_aliases=aliases or {},
        compiler_params=PARAMS,
        cost_estimate=pl.CostEstimate(flops=flops, bytes_accessed=moved, transcendentals=0),
    )(*args)


def shards(planes, pairs, activations, out_grad, weights):
    f32, bf16 = jnp.float32, jnp.bfloat16
    shape = jax.ShapeDtypeStruct
    inputs = activations[0]
    cotangent = out_grad[0]
    channels, cells = inputs.shape
    own_rows, taps, _ = weights.shape
    out = channels // (2 * planes)
    half = channels // 2
    wide = taps * out
    my_plane = lax.axis_index("dp")
    my_index = lax.axis_index("shard")
    my_pair = my_index // 2
    my_core = my_index % 2
    at_plane = my_plane.reshape(1)
    at_pair = my_pair.reshape(1)
    at_core = my_core.reshape(1)
    swap = functools.partial(exchange, planes=planes, pairs=pairs)

    def kernel_columns(core):
        start = core * half + my_plane * out
        part = lax.dynamic_slice_in_dim(weights, start, out, 2)
        return part.reshape(own_rows, wide)

    block = by_core(my_core, kernel_columns(my_core), swap(kernel_columns(1 - my_core), core=1))
    blocks = [block] + [swap(block, z=step) for step in range(1, pairs)]
    (kernel,) = call(
        functools.partial(columns_kernel, pairs, out),
        (at_pair, *blocks),
        [shape((9 * out, 3 * channels), bf16)],
        [pltpu.VMEM((channels, wide), f32)],
        0,
        scalars=1,
    )

    steps = payload_steps(planes)
    payloads = call(
        functools.partial(payload_kernel, planes, out),
        (at_plane, inputs, cotangent),
        [shape((channels + 2 * out * len(targets), cells), bf16) for targets in steps],
        [pltpu.VMEM((2, channels, cells), bf16), pltpu.SemaphoreType.DMA((2,))],
        0,
        scalars=1,
        far=(1, 2),
        spec=HBM,
    )
    own, *arrived = payloads[:1] + tuple(
        swap(payload, dp=step) for step, payload in enumerate(payloads) if step > 0
    )
    own, *arrived = lax.optimization_barrier((own, *arrived, *blocks))[: len(arrived) + 1]
    windows = [[own]] + [[part] for part in arrived]
    heights = [(channels,)] * len(windows)
    if len(windows) < planes:
        split_at = half - out
        low, high = call(
            functools.partial(halves_kernel, channels, split_at),
            arrived,
            [shape((half + out, cells), bf16)] * 2,
            [],
            0,
        )
        windows.append([swap(low, dp=2), swap(high, dp=1)])
        heights.append((split_at, channels - split_at))

    shifts = shift_matrices()
    half_flops = 2 * 2 * wide * channels * cells

    for_forward = [pltpu.VMEM((3 * channels, cells), bf16), pltpu.VMEM((9 * out, cells), f32)]
    for_gradient = [
        pltpu.VMEM((2 * SX * out, SY * SZ), bf16),
        pltpu.VMEM((2, 9 * out, cells), bf16),
    ]

    for_z = jnp.concatenate(
        [shifts[:, 3 * SY * SZ : 4 * SY * SZ], shifts[:, 5 * SY * SZ : 6 * SY * SZ]], axis=1
    )
    near = [part for ((mine,)) in windows[1:-1] for part in (mine, swap(mine, core=1))]
    a_half, total, *results = call(
        functools.partial(first_kernel, out),
        (at_core, kernel, for_z, shifts, own, swap(own, core=1), *near),
        [shape((half, channels), f32), shape((wide, channels), f32)]
        + [shape((4 * out, cells), bf16)] * (planes - 1),
        for_forward
        + [
            pltpu.VMEM((2, *own.shape), bf16),
            pltpu.SemaphoreType.DMA((3,)),
            pltpu.VMEM(shifts.shape, bf16),
        ]
        + for_gradient,
        2 * half_flops * (planes - 1),
        scalars=1,
        far=(3, 4, 5),
    )
    mine = [after(part, results[-1]) for part in windows[-1]]
    pieces = mine + [swap(part, core=1) for part in mine]
    a_half, result = call(
        functools.partial(last_kernel, out, heights[-1]),
        (at_core, kernel, for_z, *pieces, a_half),
        [shape((half, channels), f32), shape((4 * out, cells), bf16)],
        for_forward,
        half_flops,
        scalars=1,
    )
    (total,) = call(
        functools.partial(gradient_kernel, out, heights[-1]),
        (shifts, result, total, *pieces),
        [shape((wide, channels), f32)],
        [pltpu.VMEM((2, channels, cells), bf16)] + for_gradient,
        half_flops,
        aliases={2: 0},
    )
    back = [results[0]] + [
        swap(part, dp=step) for step, part in enumerate(results) if step > 0
    ]
    back = [after(part, result) for part in back] + [swap(result, dp=planes - 1)]
    theirs = [swap(after(part, total), core=1) for part in back]

    part = a_half
    for step in range(1, pairs):
        a_half = a_half + swap(part, z=step)
    a_half = after(a_half, total)

    count = planes * pairs * 2 * cells

    def inverse_of(mine):
        return call(
            functools.partial(newton_kernel, count),
            (at_core, mine, swap(mine, core=1)),
            [shape((channels, channels), f32)],
            [pltpu.VMEM((channels, channels), f32), pltpu.VMEM((2 * channels, channels), f32)],
            6 * NS_ITERS * 4 * channels**3,
            scalars=1,
        )[0]

    (g_half,) = call(
        functools.partial(gram_kernel, planes, out),
        (at_plane, at_core, *back, *theirs),
        [shape((half, channels), f32)],
        [pltpu.VMEM((channels, 2 * cells), bf16), pltpu.SemaphoreType.DMA((4 * planes,))],
        2 * 2 * half * channels * cells,
        scalars=2,
        far=range(2, 2 + 2 * planes),
    )
    inv_a = inverse_of(a_half)
    height = pairs * own_rows
    product, narrow = call(
        functools.partial(product_kernel, pairs),
        (at_core, inv_a, total, swap(total, core=1)),
        [shape((2, height, wide), f32), shape((2, height, wide), bf16)],
        [pltpu.VMEM((height, channels), f32)],
        3 * 2 * channels**2 * wide,
        scalars=1,
    )

    def part_for(array, pair):
        return lax.dynamic_slice_in_dim(array, pair * own_rows, own_rows, 1)

    block = part_for(product, my_pair)
    received = [swap(part_for(narrow, my_pair ^ step), z=step) for step in range(1, pairs)]
    for part in received:
        block = block + part.astype(f32)
    g_half = after(g_half, a_half)
    part = rows_of(g_half, my_plane, out)
    for step in range(1, planes):
        part = part + swap(rows_of(g_half, my_plane ^ step, out), dp=step)
    part = after(part, narrow)
    over_z = part
    for step in range(1, pairs):
        over_z = over_z + swap(part, z=step)
    over_z = after(over_z, received[0])
    g_half = jnp.zeros((half, channels), f32)
    for step in range(planes):
        part = over_z if step == 0 else swap(over_z, dp=step)
        g_half = place(g_half, part, my_plane ^ step)

    inv_g = inverse_of(g_half)

    block = block.astype(bf16)
    pieces = [block] + [swap(block, dp=step) for step in range(1, planes)]
    (update,) = call(
        functools.partial(update_kernel, planes, taps, out, 1.0 / math.sqrt(count)),
        (at_plane, inv_g, *pieces),
        [shape((taps * own_rows, channels), f32)],
        [pltpu.VMEM((taps * own_rows, channels), f32), pltpu.VMEM((channels, channels), f32)],
        6 * 2 * taps * own_rows * channels**2,
        scalars=1,
    )
    update = update.reshape(taps, own_rows, channels).transpose(1, 0, 2)

    (activated,) = call(
        functools.partial(sort_kernel, planes, out),
        (at_plane, at_core, *back, *theirs),
        [shape((channels, cells), bf16)],
        [pltpu.SemaphoreType.DMA((2 * planes,))],
        0,
        scalars=2,
        far=range(2, 2 + 2 * planes),
    )
    return activated[None], update


def solution(mesh):
    planes = mesh.shape["dp"]
    pairs = mesh.shape["shard"] // 2
    return jax.shard_map(
        functools.partial(shards, planes, pairs),
        mesh=mesh,
        in_specs=(
            P(("dp", "shard"), None, None),
            P(("dp", "shard"), None, None),
            P("shard", None, None),
        ),
        out_specs=(P(("dp", "shard"), None, None), P("shard", None, None)),
        check_vma=False,
    )
```
